32 devices in a mesh: chan: 4 (over y, x), pair: 8 (over z, core).
Axes of the slice: x: 2, y: 2, z: 4, core: 2. Of those that a mesh axis runs over, the one named last changes fastest.
Arguments:
- visibility: bfloat16 [4, 4096, 256], P('chan', 'pair'), may hold values from -6 to 6
- pair_counts: int32 [4096], P('pair'), may hold values from 1 to 4
- owner_ids: int32 [4096, 1], P('pair'), may hold values from 0 to 7; in each aligned block of 512 rows (0 to 511, 512 to 1023, ...) at most 132 rows name the same one
- slot_ids: int32 [4096], P('pair'), may hold values from 0 to 2047
- beam: float32 [4, 2, 2, 16384, 1024], P('chan', None, None, 'pair'), may hold values from -0.046875 to 0.046875
Outputs:
- modes: float32 [4, 1024, 2, 2, 64], P('chan', 'pair')
- mode_power: float32 [1024, 2], P('pair')
The draws below stay inside these ranges and needn't reach their ends.
Inputs may be any that keep to these rules, and one draw needn't show every extreme that they name: `owner_ids`: among the 512 feed pairs of one device, no owner is named more than 132 times, a bound that some block reaches.
All inputs are finite; a program needn't handle non-finite values.
Results may differ from the reference program's by a relative error of at most 0.0017.
Values may be sent and summed in bfloat16 or wider, within the bound.
No kernel may reach another device: no remote copies, remote signals or barrier semaphores. Data moves between devices by JAX's collectives and lax.ppermute only.
A program may use at most 64 MiB of HBM per device.

```python
import math
import jax
import jax.numpy as jnp
import numpy as np
from jax import lax

CHAN = 4
PAIR_DEV = 512
PAIRS = 4096
BASE = 16384
BASE_DEV = 2048
MODES = 1024
MWIN = 2
SETS = 64
COLS = 256
CAP = 132
N_PAIR = 8


def touch_ends(values, own_key, smallest, top_value):
    spot = [jax.random.randint(jax.random.fold_in(own_key, axis), (), 0, length) for axis, length in enumerate(values.shape)]
    longest = values.shape.index(max(values.shape))
    neighbour = spot[:longest] + [(spot[longest] + 1) % values.shape[longest]] + spot[longest + 1:]
    return values.at[tuple(spot)].set(smallest).at[tuple(neighbour)].set(top_value)


def raised(entries, own_key, source, target, blocks, factor):
    def block_of(position):
        return (jnp.arange(entries.shape[position]) // (entries.shape[position] // blocks)).reshape((-1,) + (1,) * (entries.ndim - 1 - position))

    one_side = jax.random.permutation(own_key, blocks)[block_of(target)]
    other_side = (block_of(target) + blocks // 2) % blocks
    return jnp.where((block_of(source) == one_side) | (block_of(source) == other_side), factor * entries, entries)


def shard_levels(stream_key, dims, cuts, low, high):
    level, own = 1.0, jax.random.fold_in(stream_key, 6)
    for dim, parts in cuts:
        draws = jnp.exp(jax.random.uniform(jax.random.fold_in(own, dim), (parts,), jnp.float32, low / len(cuts), high / len(cuts)))
        level = level * jnp.repeat(draws, dims[dim] // parts).reshape([-1 if axis == dim else 1 for axis in range(len(dims))])
    return level


def routed_block(stream_key, own, number, rows, number_of, top, bound, lean):
    ranking = jax.random.permutation(stream_key, number_of)
    heavy_load, ordinary = portions_of(number_of, rows * top, bound, lean, True), portions_of(number_of, rows * top, bound, lean, False)
    places = jnp.arange(number_of)

    def named(tallies, turn):
        used = int((tallies > 0).sum())
        fixed = max(1, used // 4)
        passed = fixed + (places - fixed + turn * (used - fixed)) % max(1, number_of - fixed)
        return jnp.zeros((number_of,), jnp.int32).at[ranking[jnp.where(places < fixed, places, passed)]].set(jnp.asarray(tallies, jnp.int32))

    tallies = jnp.where(number % 4 == 0, named(heavy_load, number // 4), named(ordinary, number - number // 4 - 1))
    mixed = jax.random.permutation(jax.random.fold_in(own, 3), number_of)
    giver, sink = mixed[0:number_of // 2 * 2:2], mixed[1:number_of // 2 * 2:2]
    room = jnp.minimum(tallies[giver] - 1, bound - tallies[sink]) // 2
    room = jnp.where((giver == ranking[0]) | (sink == ranking[0]) | (tallies[sink] == 0), 0, jnp.maximum(room, 0))
    passed = jax.random.randint(jax.random.fold_in(own, 4), (number_of // 2,), 0, 1 << 20) % (room + 1)
    tallies = tallies.at[giver].add(-passed).at[sink].add(passed)
    items = jnp.searchsorted(jnp.cumsum(tallies), jnp.arange(rows * top), side="right").astype(jnp.int32)
    table = items.reshape(top, rows).T
    table = table[jax.random.permutation(jax.random.fold_in(own, 1), rows)]
    turn = jax.random.randint(jax.random.fold_in(own, 2), (rows, 1), 0, top)
    return jnp.take_along_axis(table, (jnp.arange(top)[None, :] + turn) % top, axis=1)


def portions_of(count, total, limit, skew, full):
    portions = [(1 << 20) // math.isqrt(standing ** skew) + 1 for standing in range(1, count + 1)]
    largest = limit if full else min(limit, max(-(-total // count), total * portions[0] // sum(portions)))
    least = 1 if total - largest >= count - 1 else 0
    given, spare = [largest] + [least] * (count - 1), total - largest - least * (count - 1)
    while spare > 0:
        movable = [i for i in range(1, count) if given[i] < largest] or [i for i in range(1, count) if given[i] < limit]
        whole, left = sum([portions[i] for i in movable]), spare
        for i in movable:
            addition = min(limit - given[i], max(1, left * portions[i] // whole), spare)
            given[i] = given[i] + addition
            spare = spare - addition
    return np.array(given)


def centred(own_key, shape, scale, limit, cuts=(), held_as=jnp.bfloat16):
    values = jax.random.normal(own_key, shape, jnp.float32) * scale
    if len(cuts) > 0:
        values = shard_levels(own_key, shape, cuts, -0.22, 0.18) * values
    return jnp.clip(values, min=-limit, max=limit).astype(held_as)


def noise_with(key, dims, scale, bound, shards, heavy, held_as=jnp.bfloat16):
    values = scale * jax.random.normal(key, dims, jnp.float32)
    if shards:
        values = values * shard_levels(key, dims, shards, -0.22, 0.18)
    return jnp.clip(raised(values, jax.random.fold_in(key, 3), *heavy), -bound, bound).astype(held_as)


def setup_inputs(seed: int = 0) -> dict:
    streams_of = jax.random.split(jax.random.key(seed), 6)
    visibility = centred(streams_of[0], (CHAN, PAIRS, COLS), 1.0, 6.0, ((0, 4), (1, 8)))
    pair_counts = touch_ends(jax.random.randint(streams_of[1], (PAIRS,), 1, 5), jax.random.fold_in(streams_of[1], 1), 1, 4).astype(jnp.int32)
    owner_ids_keys = jax.random.split(jax.random.fold_in(streams_of[2], 1), PAIRS // PAIR_DEV)
    owner_ids_turns = jax.random.permutation(jax.random.fold_in(streams_of[2], 3), PAIRS // PAIR_DEV)
    owner_ids = jax.vmap(lambda own, number: routed_block(jax.random.fold_in(streams_of[2], 2), own, number, PAIR_DEV, N_PAIR, 1, CAP, 2))(owner_ids_keys, owner_ids_turns).reshape((PAIRS, 1))
    slot_ids = touch_ends(jax.random.randint(streams_of[3], (PAIRS,), 0, BASE_DEV), jax.random.fold_in(streams_of[3], 1), 0, BASE_DEV - 1).astype(jnp.int32)
    beam = noise_with(streams_of[4], (CHAN, MWIN, 2, BASE, MODES), (2 * BASE) ** -0.5, 0.046875, ((0, 4), (3, 8)), (3, 4, 8, 2.0), jnp.float32)
    return {"visibility": visibility, "pair_counts": pair_counts, "owner_ids": owner_ids, "slot_ids": slot_ids, "beam": beam}


def project_channel(vis_chan, beam_chan, baseline, weight, denom):
    weighted = (vis_chan.astype(jnp.float32) * weight[:, None]).astype(jnp.bfloat16)
    numer = jax.ops.segment_sum(weighted.astype(jnp.float32), baseline, num_segments=BASE)
    stacked = numer / jnp.maximum(denom, 1.0)[:, None]
    stacked = stacked.reshape(BASE, MWIN, 2, SETS)
    outputs = []
    for m_index in range(MWIN):
        real_part = stacked[:, m_index, 0, :]
        imag_part = stacked[:, m_index, 1, :]
        first = jnp.concatenate([real_part, imag_part], axis=0)
        second = jnp.concatenate([imag_part, -real_part], axis=0)
        right = jnp.concatenate([first, second], axis=1)
        left = beam_chan[m_index].reshape(2 * BASE, MODES)
        result = lax.dot_general(left, right, (((0,), (0,)), ((), ())), precision=lax.Precision.HIGHEST, preferred_element_type=jnp.float32)
        outputs.append(result.reshape(MODES, 2, SETS))
    return jnp.stack(outputs, axis=1)


def reference(visibility, pair_counts, owner_ids, slot_ids, beam):
    baseline = (owner_ids[:, 0] * BASE_DEV + slot_ids).astype(jnp.int32)
    weight = pair_counts.astype(jnp.float32)
    denom = jax.ops.segment_sum(weight, baseline, num_segments=BASE)

    def one_channel(pieces):
        return project_channel(pieces[0], pieces[1], baseline, weight, denom)

    modes = lax.map(one_channel, (visibility, beam))
    mode_power = jnp.sum(modes * modes, axis=(0, 3, 4)) / (CHAN * SETS)
    return modes, mode_power
```

```python
import functools

import jax
import jax.numpy as jnp
from jax import lax
from jax.experimental import pallas as pl
from jax.experimental.pallas import tpu as pltpu
from jax.sharding import PartitionSpec as P

MIB = 1 << 20


def round_up(value, unit):
    return -(-value // unit) * unit


def block_rows(capacity):
    first = capacity if capacity % 8 <= 5 else round_up(capacity, 8)
    return first, round_up(first + 3, 8)


def swap(value, axis, distance):
    size = lax.axis_size(axis)
    return lax.ppermute(value, axis, [(i, i ^ distance) for i in range(size)])


def pack_kernel(peers, capacity, vis_ref, counts_ref, owner_ref, slot_ref, mine_ref, theirs_ref):
    rows, columns = vis_ref.shape
    first, size = block_rows(capacity)
    padded = round_up(size, 16)
    me = lax.axis_index("pair")
    relative = owner_ref[...] ^ me
    hot = lax.broadcasted_iota(jnp.int32, (peers, rows), 0) == relative
    earlier = lax.broadcasted_iota(jnp.int32, (rows, rows), 0) < lax.broadcasted_iota(
        jnp.int32, (rows, rows), 1
    )
    counted = jnp.dot(
        jnp.where(hot, 1.0, 0.0).astype(jnp.bfloat16),
        jnp.where(earlier, 1.0, 0.0).astype(jnp.bfloat16),
        preferred_element_type=jnp.float32,
    )
    rank = jnp.sum(jnp.where(hot, counted, 0.0), axis=0, keepdims=True).astype(jnp.int32)
    slot = slot_ref[...]
    weight = counts_ref[...].astype(jnp.float32)
    line = lax.broadcasted_iota(jnp.int32, (8, rows), 0)
    facts = jnp.where(
        line == first % 8,
        (slot >> 8).astype(jnp.float32),
        jnp.where(
            line == first % 8 + 1,
            (slot & 255).astype(jnp.float32),
            jnp.where(line == first % 8 + 2, weight, 0.0),
        ),
    ).astype(jnp.bfloat16)
    places = lax.broadcasted_iota(jnp.int32, (columns, rows), 0)
    beyond = (lax.broadcasted_iota(jnp.int32, (8, columns), 0) == first % 8) & (
        lax.broadcasted_iota(jnp.int32, (8, columns), 1) >= capacity
    )
    for j in range(peers):
        match = places == jnp.where(relative == j, rank, -1)
        named = dot_rows(facts, jnp.where(match, 1.0, 0.0).astype(jnp.bfloat16))
        named = jnp.where(beyond, 255.0, named)
        scaled = jnp.where(match[:padded], weight, 0.0).astype(jnp.bfloat16)
        body = jnp.dot(scaled, vis_ref[...], preferred_element_type=jnp.float32)
        block = jnp.concatenate([body[: size - 8], body[size - 8 : size] + named], axis=0)
        out_ref = theirs_ref if j % 2 else mine_ref
        out_ref[j // 2] = block.astype(jnp.bfloat16)


def dot_rows(left, right):
    return lax.dot_general(
        left, right, (((1,), (1,)), ((), ())), preferred_element_type=jnp.float32
    )


def load_kernel(chunk, beam_ref, after_ref, high_ref, low_ref, buffer, sems):
    steps = beam_ref.shape[0] // chunk
    slots = buffer.shape[0]

    def copy(step):
        return pltpu.make_async_copy(
            beam_ref.at[pl.ds(step * chunk, chunk)],
            buffer.at[step % slots],
            sems.at[step % slots],
        )

    for step in range(min(slots, steps)):
        copy(step).start()
    for step in range(steps):
        copy(step).wait()

        @pl.loop(0, chunk // 32)
        def _(i):
            at = pl.multiple_of(i * 32, 32)
            value = buffer[step % slots, pl.ds(at, 32)]
            high = value.astype(jnp.bfloat16)
            high_ref[pl.ds(step * chunk + at, 32)] = high
            low_ref[pl.ds(step * chunk + at, 32)] = (value - high.astype(jnp.float32)).astype(
                jnp.bfloat16
            )

        if step + slots < steps:
            copy(step + slots).start()


def project_kernel(peers, capacity, mwin, *refs):
    pieces = refs[: peers // 2]
    high_ref, low_ref, keep_ref, send_ref, left_ref, total_ref = refs[peers // 2 :]
    first, size = block_rows(capacity)
    columns = pieces[0].shape[1]
    base_dev, modes = high_ref.shape[1:]
    half = columns // (2 * mwin)
    tile = 512 if base_dev % 512 == 0 else base_dev
    rows, slots, weights = [], [], []
    for piece in pieces:
        values = piece[...].astype(jnp.float32)
        rows.append(values)
        for b in range(2):
            facts = values[(b + 1) * size - 8 : (b + 1) * size].T[:size]
            high = facts[:, first % 8 : first % 8 + 1]
            low = facts[:, first % 8 + 1 : first % 8 + 2]
            slots.append((high * 256.0 + low).astype(jnp.int32))
            weights.append(jnp.broadcast_to(facts[:, first % 8 + 2 : first % 8 + 3], (size, 128)))
    rows = jnp.concatenate(rows, axis=0).T
    weights = jnp.concatenate(weights, axis=0).T[:16]
    slots = jnp.concatenate(slots, axis=0)
    left = jnp.concatenate([rows, weights], axis=0).astype(jnp.bfloat16)
    places = lax.broadcasted_iota(jnp.int32, (slots.shape[0], tile), 1)
    for n in range(base_dev // tile):
        match = jnp.where(places == slots - n * tile, 1.0, 0.0).astype(jnp.bfloat16)
        sums = jnp.dot(left, match, preferred_element_type=jnp.float32)
        stacked = sums[:columns] / jnp.maximum(sums[columns : columns + 1], 1.0)
        at_n = slice(n * tile, (n + 1) * tile)
        for m in range(mwin):
            at = 2 * half * m
            real, imag = stacked[at : at + half], stacked[at + half : at + 2 * half]
            for r, value in enumerate((stacked[at : at + 2 * half], (imag, -real))):
                if r:
                    value = jnp.concatenate(value, axis=0)
                high = value.astype(jnp.bfloat16)
                low = (value - high.astype(jnp.float32)).astype(jnp.bfloat16)
                left_ref[m, r, : 2 * half, at_n] = high
                left_ref[m, r, 2 * half :, at_n] = low
    for m in range(mwin):
        total = None
        for r in range(2):
            both = jnp.dot(
                left_ref[m, r], high_ref[2 * m + r], preferred_element_type=jnp.float32
            )
            rest = jnp.dot(
                left_ref[m, r, : 2 * half], low_ref[2 * m + r], preferred_element_type=jnp.float32
            )
            term = both[: 2 * half] + (both[2 * half :] + rest)
            total = term if total is None else total + term
        total_ref[2 * half * m : 2 * half * (m + 1)] = total
    me = lax.axis_index("pair")
    width = modes // peers
    for k in range(peers // 2):
        at = pl.multiple_of((me ^ (2 * k)) * width, width)
        keep_ref[k] = total_ref[:, pl.ds(at, width)]
        at = pl.multiple_of((me ^ (2 * k + 1)) * width, width)
        send_ref[k] = total_ref[:, pl.ds(at, width)]


def staged(visibility, pair_counts, owner_ids, slot_ids, beam):
    peers = lax.axis_size("pair")
    chips = peers // 2
    rows, columns = visibility.shape[1:]
    capacity = 2 * rows // peers + 4
    mwin, _, base_dev, modes = beam.shape[1:]
    width = modes // peers
    _, size = block_rows(capacity)
    vmem = pl.BlockSpec(memory_space=pltpu.VMEM)
    anywhere = pl.BlockSpec(memory_space=pl.ANY)
    block = jax.ShapeDtypeStruct((chips, size, columns), jnp.bfloat16)
    mine, theirs = pl.pallas_call(
        functools.partial(pack_kernel, peers, capacity),
        out_shape=(block, block),
        in_specs=[vmem] * 4,
        out_specs=(vmem, vmem),
        compiler_params=pltpu.CompilerParams(vmem_limit_bytes=8 * MIB),
        name="pack",
    )(
        visibility[0],
        pair_counts.reshape(1, rows),
        owner_ids.reshape(1, rows),
        slot_ids.reshape(1, rows),
    )
    got = swap(theirs, "pair", 1)
    pieces = [jnp.concatenate([mine[k], got[k]], axis=0) for k in range(chips)]
    moved = {k: swap(pieces[k], "pair", 2 * k) for k in reversed(range(1, chips))}
    chunk = 512
    planes = beam.reshape(mwin * 2 * base_dev, modes)
    held = pl.pallas_call(
        functools.partial(load_kernel, chunk),
        out_shape=(pltpu.VMEM(planes.shape, jnp.bfloat16),) * 2,
        in_specs=[anywhere, anywhere],
        out_specs=(vmem, vmem),
        scratch_shapes=[
            pltpu.VMEM((4, chunk, modes), jnp.float32),
            pltpu.SemaphoreType.DMA((4,)),
        ],
        compiler_params=pltpu.CompilerParams(vmem_limit_bytes=12 * MIB),
        cost_estimate=pl.CostEstimate(
            flops=0, bytes_accessed=8 * planes.size, transcendentals=0
        ),
        name="load",
    )(planes, pieces[0])
    held = [
        pltpu.with_memory_space_constraint(
            part.reshape(mwin * 2, base_dev, modes), pltpu.VMEM
        )
        for part in held
    ]
    keep, send = pl.pallas_call(
        functools.partial(project_kernel, peers, capacity, mwin),
        out_shape=(
            jax.ShapeDtypeStruct((chips, columns, width), jnp.float32),
            jax.ShapeDtypeStruct((chips, columns, width), jnp.float32),
        ),
        in_specs=[vmem] * (chips + 2),
        out_specs=(vmem, vmem),
        scratch_shapes=[
            pltpu.VMEM((mwin, 2, 2 * columns // mwin, base_dev), jnp.bfloat16),
            pltpu.VMEM((columns, modes), jnp.float32),
        ],
        compiler_params=pltpu.CompilerParams(vmem_limit_bytes=14 * MIB),
        name="project",
    )(pieces[0], *[moved[k] for k in range(1, chips)], *held)
    summed = keep + swap(send, "pair", 1)
    amplitudes = summed[0]
    for k in reversed(range(1, chips)):
        value = summed[k] if k == 1 else summed[k].astype(jnp.bfloat16)
        amplitudes = amplitudes + swap(value, "pair", 2 * k).astype(jnp.float32)
    sets = columns // (2 * mwin)
    power = jnp.sum((amplitudes * amplitudes).reshape(mwin, 2 * sets, width), axis=1)
    distance = 1
    while distance < lax.axis_size("chan"):
        power = power + swap(power, "chan", distance)
        distance *= 2
    power = power / (lax.axis_size("chan") * sets)
    shaped = amplitudes.reshape(mwin, 2, sets, width).transpose(3, 0, 1, 2)
    return shaped[None], power.T


def plain(visibility, pair_counts, owner_ids, slot_ids, beam):
    peers = lax.axis_size("pair")
    pair_rows = pair_counts.shape[0]
    capacity = 2 * pair_rows // peers + 4
    owner = owner_ids[:, 0]
    order = jnp.argsort(owner, stable=True)
    sorted_owner = owner[order]
    owner_list = jnp.arange(peers, dtype=jnp.int32)
    first_at = jnp.searchsorted(sorted_owner, owner_list, side="left")
    last_at = jnp.searchsorted(sorted_owner, owner_list, side="right")
    ranks = jnp.arange(capacity, dtype=jnp.int32)
    valid = ranks[None, :] < (last_at - first_at)[:, None]
    where_at = jnp.clip(first_at[:, None] + ranks[None, :], 0, pair_rows - 1)
    picked = order[where_at]
    weights = jnp.where(valid, pair_counts[picked], 0)
    offsets = jnp.where(valid, slot_ids[picked], 0)
    rows = visibility[0][picked]
    weighted = (rows.astype(jnp.float32) * weights[:, :, None].astype(jnp.float32)).astype(
        jnp.bfloat16
    )
    got_rows, got_offsets, got_weights = (
        lax.all_to_all(weighted, "pair", split_axis=0, concat_axis=0, tiled=True),
        lax.all_to_all(offsets, "pair", split_axis=0, concat_axis=0, tiled=True),
        lax.all_to_all(weights, "pair", split_axis=0, concat_axis=0, tiled=True),
    )
    columns = got_rows.shape[2]
    got_rows = got_rows.reshape(peers * capacity, columns)
    got_offsets = got_offsets.reshape(peers * capacity)
    got_weights = got_weights.reshape(peers * capacity).astype(jnp.float32)
    beam_local = beam[0]
    mwin = beam_local.shape[0]
    base_dev = beam_local.shape[2]
    sets = columns // (2 * mwin)
    matches = jnp.arange(base_dev, dtype=jnp.int32)[:, None] == got_offsets[None, :]
    numer = jnp.dot(matches.astype(jnp.bfloat16), got_rows, preferred_element_type=jnp.float32)
    denom = jnp.sum(jnp.where(matches, got_weights[None, :], 0.0), axis=1)
    stacked = numer / jnp.maximum(denom, 1.0)[:, None]
    stacked = stacked.reshape(base_dev, mwin, 2 * sets)
    swapped = jnp.concatenate([stacked[:, :, sets:], -stacked[:, :, :sets]], axis=2)
    right = jnp.stack([stacked, swapped], axis=0)
    amplitudes = lax.psum_scatter(
        jnp.einsum(
            "mrbk,rbmc->kmc",
            beam_local,
            right,
            precision=lax.Precision.HIGHEST,
            preferred_element_type=jnp.float32,
        ),
        "pair",
        scatter_dimension=0,
        tiled=True,
    )
    power_local = jnp.sum(amplitudes * amplitudes, axis=2)
    total_power = lax.psum(power_local, "chan")
    mode_power = total_power / (lax.axis_size("chan") * sets)
    shaped = amplitudes.reshape(amplitudes.shape[0], mwin, 2, sets)
    return (shaped[None], mode_power)


def power_of_two(value):
    return value & (value - 1) == 0


def per_device(visibility, pair_counts, owner_ids, slot_ids, beam):
    peers, channels = lax.axis_size("pair"), lax.axis_size("chan")
    rows, columns = visibility.shape[1:]
    mwin, _, base_dev, modes = beam.shape[1:]
    capacity = 2 * rows // peers + 4
    fits = (
        1 < peers <= 8
        and power_of_two(peers)
        and power_of_two(channels)
        and rows % 128 == 0
        and columns % 128 == 0
        and capacity + 8 <= columns
        and base_dev % 512 == 0
        and modes % (128 * peers) == 0
        and columns % (32 * mwin) == 0
    )
    return (staged if fits else plain)(visibility, pair_counts, owner_ids, slot_ids, beam)


def solution(mesh):
    in_specs = (
        P("chan", "pair", None),
        P("pair"),
        P("pair", None),
        P("pair"),
        P("chan", None, None, "pair", None),
    )
    out_specs = (P("chan", "pair", None, None, None), P("pair", None))
    return jax.shard_map(
        per_device, mesh=mesh, in_specs=in_specs, out_specs=out_specs, check_vma=False
    )
```

```python
import functools

import jax
import jax.numpy as jnp
from jax import lax
from jax.experimental import pallas as pl
from jax.experimental.pallas import tpu as pltpu
from jax.sharding import PartitionSpec as P

MIB = 1 << 20


def round_up(value, unit):
    return -(-value // unit) * unit


def block_rows(capacity):
    first = capacity if capacity % 8 <= 5 else round_up(capacity, 8)
    return first, round_up(first + 3, 8)


def swap(value, axis, distance):
    size = lax.axis_size(axis)
    return lax.ppermute(value, axis, [(i, i ^ distance) for i in range(size)])


def pack_kernel(peers, capacity, *refs):
    sources, (mine_ref, theirs_ref), held, sems = refs[:4], refs[4:6], refs[6:10], refs[10]
    copies = [
        pltpu.make_async_copy(source, target, sems.at[i])
        for i, (source, target) in enumerate(zip(sources, held))
    ]
    for copy in copies:
        copy.start()
    for copy in copies:
        copy.wait()
    vis_ref, counts_ref, owner_ref, slot_ref = held
    rows, columns = vis_ref.shape
    first, size = block_rows(capacity)
    padded = round_up(size, 16)
    me = lax.axis_index("pair")
    relative = owner_ref[...] ^ me
    hot = lax.broadcasted_iota(jnp.int32, (peers, rows), 0) == relative
    earlier = lax.broadcasted_iota(jnp.int32, (rows, rows), 0) < lax.broadcasted_iota(
        jnp.int32, (rows, rows), 1
    )
    counted = jnp.dot(
        jnp.where(hot, 1.0, 0.0).astype(jnp.bfloat16),
        jnp.where(earlier, 1.0, 0.0).astype(jnp.bfloat16),
        preferred_element_type=jnp.float32,
    )
    rank = jnp.sum(jnp.where(hot, counted, 0.0), axis=0, keepdims=True).astype(jnp.int32)
    slot = slot_ref[...]
    weight = counts_ref[...].astype(jnp.float32)
    line = lax.broadcasted_iota(jnp.int32, (8, rows), 0)
    facts = jnp.where(
        line == first % 8,
        (slot >> 8).astype(jnp.float32),
        jnp.where(
            line == first % 8 + 1,
            (slot & 255).astype(jnp.float32),
            jnp.where(line == first % 8 + 2, weight, 0.0),
        ),
    ).astype(jnp.bfloat16)
    places = lax.broadcasted_iota(jnp.int32, (columns, rows), 0)
    beyond = (lax.broadcasted_iota(jnp.int32, (8, columns), 0) == first % 8) & (
        lax.broadcasted_iota(jnp.int32, (8, columns), 1) >= capacity
    )
    for j in range(peers):
        match = places == jnp.where(relative == j, rank, -1)
        named = dot_rows(facts, jnp.where(match, 1.0, 0.0).astype(jnp.bfloat16))
        named = jnp.where(beyond, 255.0, named)
        scaled = jnp.where(match[:padded], weight, 0.0).astype(jnp.bfloat16)
        body = jnp.dot(scaled, vis_ref[...], preferred_element_type=jnp.float32)
        block = jnp.concatenate([body[: size - 8], body[size - 8 : size] + named], axis=0)
        out_ref = theirs_ref if j % 2 else mine_ref
        out_ref[j // 2] = block.astype(jnp.bfloat16)


def dot_rows(left, right):
    return lax.dot_general(
        left, right, (((1,), (1,)), ((), ())), preferred_element_type=jnp.float32
    )


def load_kernel(peers, chunk, beam_ref, after_ref, *refs):
    outs, buffer, sems = (refs[:2], refs[2:4]), refs[4], refs[5]
    steps = beam_ref.shape[0] // chunk
    slots = buffer.shape[0]
    width = beam_ref.shape[1] // peers
    me = lax.axis_index("pair")

    def copy(step):
        return pltpu.make_async_copy(
            beam_ref.at[pl.ds(step * chunk, chunk)],
            buffer.at[step % slots],
            sems.at[step % slots],
        )

    for step in range(min(slots, steps)):
        copy(step).start()
    for step in range(steps):
        copy(step).wait()

        @pl.loop(0, chunk // 32)
        def _(i):
            at = pl.multiple_of(i * 32, 32)
            for j in range(peers):
                lane = pl.multiple_of((me ^ j) * width, width)
                value = buffer[step % slots, pl.ds(at, 32), pl.ds(lane, width)]
                high = value.astype(jnp.bfloat16)
                low = (value - high.astype(jnp.float32)).astype(jnp.bfloat16)
                high_ref, low_ref = outs[1 - j % 2]
                to = (pl.ds(step * chunk + at, 32), slice(j // 2 * width, (j // 2 + 1) * width))
                high_ref[to] = high
                low_ref[to] = low

        if step + slots < steps:
            copy(step + slots).start()


def stack_kernel(peers, capacity, mwin, *refs):
    pieces = refs[: peers // 2]
    high_ref, low_ref, left_ref, send_ref = refs[peers // 2 :]
    first, size = block_rows(capacity)
    columns = pieces[0].shape[1]
    base_dev = left_ref.shape[3]
    half = columns // (2 * mwin)
    tile = 512 if base_dev % 512 == 0 else base_dev
    rows, slots, weights = [], [], []
    for piece in pieces:
        values = piece[...].astype(jnp.float32)
        rows.append(values)
        for b in range(2):
            facts = values[(b + 1) * size - 8 : (b + 1) * size].T[:size]
            high = facts[:, first % 8 : first % 8 + 1]
            low = facts[:, first % 8 + 1 : first % 8 + 2]
            slots.append((high * 256.0 + low).astype(jnp.int32))
            weights.append(jnp.broadcast_to(facts[:, first % 8 + 2 : first % 8 + 3], (size, 128)))
    rows = jnp.concatenate(rows, axis=0).T
    weights = jnp.concatenate(weights, axis=0).T[:16]
    slots = jnp.concatenate(slots, axis=0)
    left = jnp.concatenate([rows, weights], axis=0).astype(jnp.bfloat16)
    places = lax.broadcasted_iota(jnp.int32, (slots.shape[0], tile), 1)
    for n in range(base_dev // tile):
        match = jnp.where(places == slots - n * tile, 1.0, 0.0).astype(jnp.bfloat16)
        sums = jnp.dot(left, match, preferred_element_type=jnp.float32)
        stacked = sums[:columns] / jnp.maximum(sums[columns : columns + 1], 1.0)
        at_n = slice(n * tile, (n + 1) * tile)
        for m in range(mwin):
            at = 2 * half * m
            real, imag = stacked[at : at + half], stacked[at + half : at + 2 * half]
            for r, value in enumerate((stacked[at : at + 2 * half], (imag, -real))):
                if r:
                    value = jnp.concatenate(value, axis=0)
                high = value.astype(jnp.bfloat16)
                low = (value - high.astype(jnp.float32)).astype(jnp.bfloat16)
                left_ref[m, r, : 2 * half, at_n] = high
                left_ref[m, r, 2 * half :, at_n] = low
    project(left_ref, high_ref, low_ref, send_ref)


def project(left_ref, high_ref, low_ref, out_ref):
    mwin, _, rows, base_dev = left_ref.shape
    half = rows // 2
    chips, _, width = out_ref.shape
    for m in range(mwin):
        total = None
        for r in range(2):
            plane = slice((2 * m + r) * base_dev, (2 * m + r + 1) * base_dev)
            both = jnp.dot(
                left_ref[m, r], high_ref[plane], preferred_element_type=jnp.float32
            )
            rest = jnp.dot(
                left_ref[m, r, :half], low_ref[plane], preferred_element_type=jnp.float32
            )
            term = both[:half] + (both[half:] + rest)
            total = term if total is None else total + term
        for k in range(chips):
            out_ref[k, m * half : (m + 1) * half] = total[:, k * width : (k + 1) * width]


def keep_kernel(left_ref, high_ref, low_ref, keep_ref):
    project(left_ref, high_ref, low_ref, keep_ref)


def staged(visibility, pair_counts, owner_ids, slot_ids, beam):
    peers = lax.axis_size("pair")
    chips = peers // 2
    rows, columns = visibility.shape[1:]
    capacity = 2 * rows // peers + 4
    mwin, _, base_dev, modes = beam.shape[1:]
    width = modes // peers
    _, size = block_rows(capacity)
    vmem = pl.BlockSpec(memory_space=pltpu.VMEM)
    anywhere = pl.BlockSpec(memory_space=pl.ANY)
    block = jax.ShapeDtypeStruct((chips, size, columns), jnp.bfloat16)
    facts = [value.reshape(1, rows) for value in (pair_counts, owner_ids, slot_ids)]
    mine, theirs = pl.pallas_call(
        functools.partial(pack_kernel, peers, capacity),
        out_shape=(block, block),
        in_specs=[anywhere] * 4,
        out_specs=(vmem, vmem),
        scratch_shapes=[pltpu.VMEM((rows, columns), jnp.bfloat16)]
        + [pltpu.VMEM((1, rows), jnp.int32)] * 3
        + [pltpu.SemaphoreType.DMA((4,))],
        compiler_params=pltpu.CompilerParams(vmem_limit_bytes=8 * MIB),
        name="pack",
    )(*[pltpu.with_memory_space_constraint(value, pltpu.HBM) for value in (visibility[0], *facts)])
    got = swap(theirs, "pair", 1)
    pieces = [jnp.concatenate([mine[k], got[k]], axis=0) for k in range(chips)]
    order = [k for k in range(1, chips) if k & (chips // 2)] + [
        k for k in range(1, chips) if not k & (chips // 2)
    ]
    moved = {k: swap(pieces[k], "pair", 2 * k) for k in order}
    chunk = 512
    planes = beam.reshape(mwin * 2 * base_dev, modes)
    held = pl.pallas_call(
        functools.partial(load_kernel, peers, chunk),
        out_shape=(pltpu.VMEM((planes.shape[0], modes // 2), jnp.bfloat16),) * 4,
        in_specs=[anywhere, anywhere],
        out_specs=(vmem,) * 4,
        scratch_shapes=[
            pltpu.VMEM((4, chunk, modes), jnp.float32),
            pltpu.SemaphoreType.DMA((4,)),
        ],
        compiler_params=pltpu.CompilerParams(vmem_limit_bytes=12 * MIB),
        cost_estimate=pl.CostEstimate(
            flops=0, bytes_accessed=8 * planes.size, transcendentals=0
        ),
        name="load",
    )(planes, pieces[0])
    held = [pltpu.with_memory_space_constraint(part, pltpu.VMEM) for part in held]
    products = jax.ShapeDtypeStruct((chips, columns, width), jnp.float32)
    flops = 6 * mwin * 2 * (columns // mwin) * base_dev * modes // 2
    left, send = pl.pallas_call(
        functools.partial(stack_kernel, peers, capacity, mwin),
        out_shape=(
            pltpu.VMEM((mwin, 2, 2 * columns // mwin, base_dev), jnp.bfloat16),
            products,
        ),
        in_specs=[vmem] * (chips + 2),
        out_specs=(vmem, vmem),
        compiler_params=pltpu.CompilerParams(vmem_limit_bytes=12 * MIB),
        cost_estimate=pl.CostEstimate(flops=flops, bytes_accessed=0, transcendentals=0),
        name="stack",
    )(pieces[0], *[moved[k] for k in order], *held[:2])
    got = swap(send, "pair", 1)
    keep = pl.pallas_call(
        keep_kernel,
        out_shape=products,
        in_specs=[vmem] * 3,
        out_specs=vmem,
        compiler_params=pltpu.CompilerParams(vmem_limit_bytes=12 * MIB),
        cost_estimate=pl.CostEstimate(flops=flops, bytes_accessed=0, transcendentals=0),
        name="keep",
    )(pltpu.with_memory_space_constraint(left, pltpu.VMEM), *held[2:])
    summed = keep + got
    amplitudes = summed[0]
    for k in order:
        value = summed[k] if k == 1 else summed[k].astype(jnp.bfloat16)
        amplitudes = amplitudes + swap(value, "pair", 2 * k).astype(jnp.float32)
    sets = columns // (2 * mwin)
    power = jnp.sum((amplitudes * amplitudes).reshape(mwin, 2 * sets, width), axis=1)
    distance = 1
    while distance < lax.axis_size("chan"):
        power = power + swap(power, "chan", distance)
        distance *= 2
    power = power / (lax.axis_size("chan") * sets)
    shaped = amplitudes.reshape(mwin, 2, sets, width).transpose(3, 0, 1, 2)
    return shaped[None], power.T


def plain(visibility, pair_counts, owner_ids, slot_ids, beam):
    peers = lax.axis_size("pair")
    pair_rows = pair_counts.shape[0]
    capacity = 2 * pair_rows // peers + 4
    owner = owner_ids[:, 0]
    order = jnp.argsort(owner, stable=True)
    sorted_owner = owner[order]
    owner_list = jnp.arange(peers, dtype=jnp.int32)
    first_at = jnp.searchsorted(sorted_owner, owner_list, side="left")
    last_at = jnp.searchsorted(sorted_owner, owner_list, side="right")
    ranks = jnp.arange(capacity, dtype=jnp.int32)
    valid = ranks[None, :] < (last_at - first_at)[:, None]
    where_at = jnp.clip(first_at[:, None] + ranks[None, :], 0, pair_rows - 1)
    picked = order[where_at]
    weights = jnp.where(valid, pair_counts[picked], 0)
    offsets = jnp.where(valid, slot_ids[picked], 0)
    rows = visibility[0][picked]
    weighted = (rows.astype(jnp.float32) * weights[:, :, None].astype(jnp.float32)).astype(
        jnp.bfloat16
    )
    got_rows, got_offsets, got_weights = (
        lax.all_to_all(weighted, "pair", split_axis=0, concat_axis=0, tiled=True),
        lax.all_to_all(offsets, "pair", split_axis=0, concat_axis=0, tiled=True),
        lax.all_to_all(weights, "pair", split_axis=0, concat_axis=0, tiled=True),
    )
    columns = got_rows.shape[2]
    got_rows = got_rows.reshape(peers * capacity, columns)
    got_offsets = got_offsets.reshape(peers * capacity)
    got_weights = got_weights.reshape(peers * capacity).astype(jnp.float32)
    beam_local = beam[0]
    mwin = beam_local.shape[0]
    base_dev = beam_local.shape[2]
    sets = columns // (2 * mwin)
    matches = jnp.arange(base_dev, dtype=jnp.int32)[:, None] == got_offsets[None, :]
    numer = jnp.dot(matches.astype(jnp.bfloat16), got_rows, preferred_element_type=jnp.float32)
    denom = jnp.sum(jnp.where(matches, got_weights[None, :], 0.0), axis=1)
    stacked = numer / jnp.maximum(denom, 1.0)[:, None]
    stacked = stacked.reshape(base_dev, mwin, 2 * sets)
    swapped = jnp.concatenate([stacked[:, :, sets:], -stacked[:, :, :sets]], axis=2)
    right = jnp.stack([stacked, swapped], axis=0)
    amplitudes = lax.psum_scatter(
        jnp.einsum(
            "mrbk,rbmc->kmc",
            beam_local,
            right,
            precision=lax.Precision.HIGHEST,
            preferred_element_type=jnp.float32,
        ),
        "pair",
        scatter_dimension=0,
        tiled=True,
    )
    power_local = jnp.sum(amplitudes * amplitudes, axis=2)
    total_power = lax.psum(power_local, "chan")
    mode_power = total_power / (lax.axis_size("chan") * sets)
    shaped = amplitudes.reshape(amplitudes.shape[0], mwin, 2, sets)
    return (shaped[None], mode_power)


def power_of_two(value):
    return value & (value - 1) == 0


def per_device(visibility, pair_counts, owner_ids, slot_ids, beam):
    peers, channels = lax.axis_size("pair"), lax.axis_size("chan")
    rows, columns = visibility.shape[1:]
    mwin, _, base_dev, modes = beam.shape[1:]
    capacity = 2 * rows // peers + 4
    fits = (
        1 < peers <= 8
        and power_of_two(peers)
        and power_of_two(channels)
        and rows % 128 == 0
        and columns % 128 == 0
        and capacity + 8 <= columns
        and base_dev % 512 == 0
        and modes % (128 * peers) == 0
        and columns % (32 * mwin) == 0
    )
    return (staged if fits else plain)(visibility, pair_counts, owner_ids, slot_ids, beam)


def solution(mesh):
    in_specs = (
        P("chan", "pair", None),
        P("pair"),
        P("pair", None),
        P("pair"),
        P("chan", None, None, "pair", None),
    )
    out_specs = (P("chan", "pair", None, None, None), P("pair", None))
    return jax.shard_map(
        per_device, mesh=mesh, in_specs=in_specs, out_specs=out_specs, check_vma=False
    )
```

```python
import functools

import jax
import jax.numpy as jnp
from jax import lax
from jax.experimental import pallas as pl
from jax.experimental.pallas import tpu as pltpu
from jax.sharding import PartitionSpec as P

MIB = 1 << 20


def round_up(value, unit):
    return -(-value // unit) * unit


def block_rows(capacity):
    first = capacity if capacity % 8 <= 5 else round_up(capacity, 8)
    return first, round_up(first + 3, 8)


def swap(value, axis, distance):
    size = lax.axis_size(axis)
    return lax.ppermute(value, axis, [(i, i ^ distance) for i in range(size)])


def pack_kernel(peers, capacity, *refs):
    sources, (mine_ref, theirs_ref), held, sems = refs[:4], refs[4:6], refs[6:10], refs[10]
    copies = [
        pltpu.make_async_copy(source, target, sems.at[i])
        for i, (source, target) in enumerate(zip(sources, held))
    ]
    for copy in copies:
        copy.start()
    for copy in copies:
        copy.wait()
    vis_ref, counts_ref, owner_ref, slot_ref = held
    rows, columns = vis_ref.shape
    first, size = block_rows(capacity)
    padded = round_up(size, 16)
    me = lax.axis_index("pair")
    relative = owner_ref[...] ^ me
    hot = lax.broadcasted_iota(jnp.int32, (peers, rows), 0) == relative
    earlier = lax.broadcasted_iota(jnp.int32, (rows, rows), 0) < lax.broadcasted_iota(
        jnp.int32, (rows, rows), 1
    )
    counted = jnp.dot(
        jnp.where(hot, 1.0, 0.0).astype(jnp.bfloat16),
        jnp.where(earlier, 1.0, 0.0).astype(jnp.bfloat16),
        preferred_element_type=jnp.float32,
    )
    rank = jnp.sum(jnp.where(hot, counted, 0.0), axis=0, keepdims=True).astype(jnp.int32)
    slot = slot_ref[...]
    weight = counts_ref[...].astype(jnp.float32)
    line = lax.broadcasted_iota(jnp.int32, (8, rows), 0)
    facts = jnp.where(
        line == first % 8,
        (slot >> 8).astype(jnp.float32),
        jnp.where(
            line == first % 8 + 1,
            (slot & 255).astype(jnp.float32),
            jnp.where(line == first % 8 + 2, weight, 0.0),
        ),
    ).astype(jnp.bfloat16)
    places = lax.broadcasted_iota(jnp.int32, (columns, rows), 0)
    beyond = (lax.broadcasted_iota(jnp.int32, (8, columns), 0) == first % 8) & (
        lax.broadcasted_iota(jnp.int32, (8, columns), 1) >= capacity
    )
    for j in range(peers):
        match = places == jnp.where(relative == j, rank, -1)
        named = dot_rows(facts, jnp.where(match, 1.0, 0.0).astype(jnp.bfloat16))
        named = jnp.where(beyond, 255.0, named)
        scaled = jnp.where(match[:padded], weight, 0.0).astype(jnp.bfloat16)
        body = jnp.dot(scaled, vis_ref[...], preferred_element_type=jnp.float32)
        block = jnp.concatenate([body[: size - 8], body[size - 8 : size] + named], axis=0)
        out_ref = theirs_ref if j % 2 else mine_ref
        out_ref[j // 2] = block.astype(jnp.bfloat16)


def dot_rows(left, right):
    return lax.dot_general(
        left, right, (((1,), (1,)), ((), ())), preferred_element_type=jnp.float32
    )


def groups(peers):
    chips = peers // 2
    return (
        [2 * k + 1 for k in range(chips)],
        [2 * k for k in range(chips) if k & (chips // 2)],
        [2 * k for k in range(chips) if not k & (chips // 2)],
    )


def load_kernel(peers, chunk, beam_ref, after_ref, *refs):
    outs, buffer, sems = (refs[:2], refs[2:4], refs[4:6]), refs[6], refs[7]
    steps = beam_ref.shape[0] // chunk
    slots = buffer.shape[0]
    width = beam_ref.shape[1] // peers
    me = lax.axis_index("pair")

    def copy(step):
        return pltpu.make_async_copy(
            beam_ref.at[pl.ds(step * chunk, chunk)],
            buffer.at[step % slots],
            sems.at[step % slots],
        )

    for step in range(min(slots, steps)):
        copy(step).start()
    for step in range(steps):
        copy(step).wait()

        @pl.loop(0, chunk // 32)
        def _(line):
            at = pl.multiple_of(line * 32, 32)
            for (high_ref, low_ref), owners in zip(outs, groups(peers)):
                for i, j in enumerate(owners):
                    lane = pl.multiple_of((me ^ j) * width, width)
                    value = buffer[step % slots, pl.ds(at, 32), pl.ds(lane, width)]
                    high = value.astype(jnp.bfloat16)
                    low = (value - high.astype(jnp.float32)).astype(jnp.bfloat16)
                    to = (pl.ds(step * chunk + at, 32), slice(i * width, (i + 1) * width))
                    high_ref[to] = high
                    low_ref[to] = low

        if step + slots < steps:
            copy(step + slots).start()


def stack_kernel(peers, capacity, mwin, *refs):
    pieces = refs[: peers // 2]
    high_ref, low_ref, left_ref, send_ref = refs[peers // 2 :]
    first, size = block_rows(capacity)
    columns = pieces[0].shape[1]
    base_dev = left_ref.shape[3]
    half = columns // (2 * mwin)
    tile = 512 if base_dev % 512 == 0 else base_dev
    rows, slots, weights = [], [], []
    for piece in pieces:
        values = piece[...].astype(jnp.float32)
        rows.append(values)
        for b in range(2):
            facts = values[(b + 1) * size - 8 : (b + 1) * size].T[:size]
            high = facts[:, first % 8 : first % 8 + 1]
            low = facts[:, first % 8 + 1 : first % 8 + 2]
            slots.append((high * 256.0 + low).astype(jnp.int32))
            weights.append(jnp.broadcast_to(facts[:, first % 8 + 2 : first % 8 + 3], (size, 128)))
    rows = jnp.concatenate(rows, axis=0).T
    weights = jnp.concatenate(weights, axis=0).T[:16]
    slots = jnp.concatenate(slots, axis=0)
    left = jnp.concatenate([rows, weights], axis=0).astype(jnp.bfloat16)
    places = lax.broadcasted_iota(jnp.int32, (slots.shape[0], tile), 1)
    for n in range(base_dev // tile):
        match = jnp.where(places == slots - n * tile, 1.0, 0.0).astype(jnp.bfloat16)
        sums = jnp.dot(left, match, preferred_element_type=jnp.float32)
        stacked = sums[:columns] / jnp.maximum(sums[columns : columns + 1], 1.0)
        at_n = slice(n * tile, (n + 1) * tile)
        for m in range(mwin):
            at = 2 * half * m
            real, imag = stacked[at : at + half], stacked[at + half : at + 2 * half]
            for r, value in enumerate((stacked[at : at + 2 * half], (imag, -real))):
                if r:
                    value = jnp.concatenate(value, axis=0)
                high = value.astype(jnp.bfloat16)
                low = (value - high.astype(jnp.float32)).astype(jnp.bfloat16)
                left_ref[m, r, : 2 * half, at_n] = high
                left_ref[m, r, 2 * half :, at_n] = low
    project(left_ref, high_ref, low_ref, send_ref)


def project(left_ref, high_ref, low_ref, out_ref):
    mwin, _, rows, base_dev = left_ref.shape
    half = rows // 2
    chips, _, width = out_ref.shape
    for m in range(mwin):
        total = None
        for r in range(2):
            plane = slice((2 * m + r) * base_dev, (2 * m + r + 1) * base_dev)
            both = jnp.dot(
                left_ref[m, r], high_ref[plane], preferred_element_type=jnp.float32
            )
            rest = jnp.dot(
                left_ref[m, r, :half], low_ref[plane], preferred_element_type=jnp.float32
            )
            term = both[:half] + (both[half:] + rest)
            total = term if total is None else total + term
        for k in range(chips):
            out_ref[k, m * half : (m + 1) * half] = total[:, k * width : (k + 1) * width]


def keep_kernel(left_ref, high_ref, low_ref, *refs):
    keep_ref = refs[-1]
    project(left_ref, high_ref, low_ref, keep_ref)


def staged(visibility, pair_counts, owner_ids, slot_ids, beam):
    peers = lax.axis_size("pair")
    chips = peers // 2
    rows, columns = visibility.shape[1:]
    capacity = 2 * rows // peers + 4
    mwin, _, base_dev, modes = beam.shape[1:]
    width = modes // peers
    _, size = block_rows(capacity)
    vmem = pl.BlockSpec(memory_space=pltpu.VMEM)
    anywhere = pl.BlockSpec(memory_space=pl.ANY)
    block = jax.ShapeDtypeStruct((chips, size, columns), jnp.bfloat16)
    facts = [value.reshape(1, rows) for value in (pair_counts, owner_ids, slot_ids)]
    mine, theirs = pl.pallas_call(
        functools.partial(pack_kernel, peers, capacity),
        out_shape=(block, block),
        in_specs=[anywhere] * 4,
        out_specs=(vmem, vmem),
        scratch_shapes=[pltpu.VMEM((rows, columns), jnp.bfloat16)]
        + [pltpu.VMEM((1, rows), jnp.int32)] * 3
        + [pltpu.SemaphoreType.DMA((4,))],
        compiler_params=pltpu.CompilerParams(vmem_limit_bytes=8 * MIB),
        name="pack",
    )(*[pltpu.with_memory_space_constraint(value, pltpu.HBM) for value in (visibility[0], *facts)])
    got = swap(theirs, "pair", 1)
    pieces = [jnp.concatenate([mine[k], got[k]], axis=0) for k in range(chips)]
    order = [k for k in range(1, chips) if k & (chips // 2)] + [
        k for k in range(1, chips) if not k & (chips // 2)
    ]
    moved = {k: swap(pieces[k], "pair", 2 * k) for k in order}
    chunk = 512
    planes = beam.reshape(mwin * 2 * base_dev, modes)
    held = pl.pallas_call(
        functools.partial(load_kernel, peers, chunk),
        out_shape=tuple(
            pltpu.VMEM((planes.shape[0], len(owners) * width), jnp.bfloat16)
            for owners in groups(peers)
            for _ in range(2)
        ),
        in_specs=[anywhere, anywhere],
        out_specs=(vmem,) * 6,
        scratch_shapes=[
            pltpu.VMEM((4, chunk, modes), jnp.float32),
            pltpu.SemaphoreType.DMA((4,)),
        ],
        compiler_params=pltpu.CompilerParams(vmem_limit_bytes=12 * MIB),
        cost_estimate=pl.CostEstimate(
            flops=0, bytes_accessed=8 * planes.size, transcendentals=0
        ),
        name="load",
    )(planes, pieces[0])
    held = [pltpu.with_memory_space_constraint(part, pltpu.VMEM) for part in held]
    def products(count):
        return jax.ShapeDtypeStruct((count, columns, width), jnp.float32)

    def cost(count):
        flops = 6 * mwin * 2 * (columns // mwin) * base_dev * count * width
        return pl.CostEstimate(flops=flops, bytes_accessed=0, transcendentals=0)

    left, send = pl.pallas_call(
        functools.partial(stack_kernel, peers, capacity, mwin),
        out_shape=(
            pltpu.VMEM((mwin, 2, 2 * columns // mwin, base_dev), jnp.bfloat16),
            products(chips),
        ),
        in_specs=[vmem] * (chips + 2),
        out_specs=(vmem, vmem),
        compiler_params=pltpu.CompilerParams(vmem_limit_bytes=12 * MIB),
        cost_estimate=cost(chips),
        name="stack",
    )(pieces[0], *[moved[k] for k in order], *held[:2])
    got = swap(send, "pair", 1)
    left = pltpu.with_memory_space_constraint(left, pltpu.VMEM)
    summed, after = {}, []
    for name, parts, owners in zip(("far", "near"), (held[2:4], held[4:6]), groups(peers)[1:]):
        keep = pl.pallas_call(
            keep_kernel,
            out_shape=products(len(owners)),
            in_specs=[vmem] * 3 + [anywhere] * len(after),
            out_specs=vmem,
            compiler_params=pltpu.CompilerParams(vmem_limit_bytes=12 * MIB),
            cost_estimate=cost(len(owners)),
            name=name,
        )(left, *parts, *after)
        for i, j in enumerate(owners):
            k = j // 2
            summed[k] = keep[i] + got[k]
            if k:
                summed[k] = summed[k].astype(jnp.bfloat16)
            if k & (chips // 2):
                after.append(summed[k])
    amplitudes = summed[0]
    for k in order:
        if not k & (chips // 2):
            amplitudes = lax.optimization_barrier(amplitudes)
        amplitudes = amplitudes + swap(summed[k], "pair", 2 * k).astype(jnp.float32)
    sets = columns // (2 * mwin)
    power = jnp.sum((amplitudes * amplitudes).reshape(mwin, 2 * sets, width), axis=1)
    distance = 1
    while distance < lax.axis_size("chan"):
        power = power + swap(power, "chan", distance)
        distance *= 2
    power = power / (lax.axis_size("chan") * sets)
    shaped = amplitudes.reshape(mwin, 2, sets, width).transpose(3, 0, 1, 2)
    return shaped[None], power.T


def plain(visibility, pair_counts, owner_ids, slot_ids, beam):
    peers = lax.axis_size("pair")
    pair_rows = pair_counts.shape[0]
    capacity = 2 * pair_rows // peers + 4
    owner = owner_ids[:, 0]
    order = jnp.argsort(owner, stable=True)
    sorted_owner = owner[order]
    owner_list = jnp.arange(peers, dtype=jnp.int32)
    first_at = jnp.searchsorted(sorted_owner, owner_list, side="left")
    last_at = jnp.searchsorted(sorted_owner, owner_list, side="right")
    ranks = jnp.arange(capacity, dtype=jnp.int32)
    valid = ranks[None, :] < (last_at - first_at)[:, None]
    where_at = jnp.clip(first_at[:, None] + ranks[None, :], 0, pair_rows - 1)
    picked = order[where_at]
    weights = jnp.where(valid, pair_counts[picked], 0)
    offsets = jnp.where(valid, slot_ids[picked], 0)
    rows = visibility[0][picked]
    weighted = (rows.astype(jnp.float32) * weights[:, :, None].astype(jnp.float32)).astype(
        jnp.bfloat16
    )
    got_rows, got_offsets, got_weights = (
        lax.all_to_all(weighted, "pair", split_axis=0, concat_axis=0, tiled=True),
        lax.all_to_all(offsets, "pair", split_axis=0, concat_axis=0, tiled=True),
        lax.all_to_all(weights, "pair", split_axis=0, concat_axis=0, tiled=True),
    )
    columns = got_rows.shape[2]
    got_rows = got_rows.reshape(peers * capacity, columns)
    got_offsets = got_offsets.reshape(peers * capacity)
    got_weights = got_weights.reshape(peers * capacity).astype(jnp.float32)
    beam_local = beam[0]
    mwin = beam_local.shape[0]
    base_dev = beam_local.shape[2]
    sets = columns // (2 * mwin)
    matches = jnp.arange(base_dev, dtype=jnp.int32)[:, None] == got_offsets[None, :]
    numer = jnp.dot(matches.astype(jnp.bfloat16), got_rows, preferred_element_type=jnp.float32)
    denom = jnp.sum(jnp.where(matches, got_weights[None, :], 0.0), axis=1)
    stacked = numer / jnp.maximum(denom, 1.0)[:, None]
    stacked = stacked.reshape(base_dev, mwin, 2 * sets)
    swapped = jnp.concatenate([stacked[:, :, sets:], -stacked[:, :, :sets]], axis=2)
    right = jnp.stack([stacked, swapped], axis=0)
    amplitudes = lax.psum_scatter(
        jnp.einsum(
            "mrbk,rbmc->kmc",
            beam_local,
            right,
            precision=lax.Precision.HIGHEST,
            preferred_element_type=jnp.float32,
        ),
        "pair",
        scatter_dimension=0,
        tiled=True,
    )
    power_local = jnp.sum(amplitudes * amplitudes, axis=2)
    total_power = lax.psum(power_local, "chan")
    mode_power = total_power / (lax.axis_size("chan") * sets)
    shaped = amplitudes.reshape(amplitudes.shape[0], mwin, 2, sets)
    return (shaped[None], mode_power)


def power_of_two(value):
    return value & (value - 1) == 0


def per_device(visibility, pair_counts, owner_ids, slot_ids, beam):
    peers, channels = lax.axis_size("pair"), lax.axis_size("chan")
    rows, columns = visibility.shape[1:]
    mwin, _, base_dev, modes = beam.shape[1:]
    capacity = 2 * rows // peers + 4
    fits = (
        1 < peers <= 8
        and power_of_two(peers)
        and power_of_two(channels)
        and rows % 128 == 0
        and columns % 128 == 0
        and capacity + 8 <= columns
        and base_dev % 512 == 0
        and modes % (128 * peers) == 0
        and columns % (32 * mwin) == 0
    )
    return (staged if fits else plain)(visibility, pair_counts, owner_ids, slot_ids, beam)


def solution(mesh):
    in_specs = (
        P("chan", "pair", None),
        P("pair"),
        P("pair", None),
        P("pair"),
        P("chan", None, None, "pair", None),
    )
    out_specs = (P("chan", "pair", None, None, None), P("pair", None))
    return jax.shard_map(
        per_device, mesh=mesh, in_specs=in_specs, out_specs=out_specs, check_vma=False
    )
```

```python
import functools

import jax
import jax.numpy as jnp
from jax import lax
from jax.experimental import pallas as pl
from jax.experimental.pallas import tpu as pltpu
from jax.sharding import PartitionSpec as P

MIB = 1 << 20
SMALL = jnp.float8_e5m2
AHEAD = 2
BEAM, BEAM_REST, STACK, STACK_REST = 2.0**18, 2.0**27, 2.0**12, 2.0**21


def round_up(value, unit):
    return -(-value // unit) * unit


def block_rows(capacity):
    first = capacity if capacity % 8 <= 5 else round_up(capacity, 8)
    return first, round_up(first + 3, 8)


def swap(value, axis, distance):
    size = lax.axis_size(axis)
    return lax.ppermute(value, axis, [(i, i ^ distance) for i in range(size)])


def pack_kernel(peers, capacity, *refs):
    sources, beam_ref, (mine_ref, theirs_ref, start_ref) = refs[:4], refs[4], refs[5:8]
    held, sems = refs[8:12], refs[12]
    copies = [
        pltpu.make_async_copy(source, target, sems.at[i])
        for i, (source, target) in enumerate(zip(sources, held))
    ]
    for copy in copies:
        copy.start()
    ahead = pltpu.make_async_copy(beam_ref.at[pl.ds(0, start_ref.shape[0])], start_ref, sems.at[4])
    ahead.start()
    for copy in copies:
        copy.wait()
    vis_ref, counts_ref, owner_ref, slot_ref = held
    rows, columns = vis_ref.shape
    first, size = block_rows(capacity)
    padded = round_up(size, 16)
    me = lax.axis_index("pair")
    relative = owner_ref[...] ^ me
    hot = lax.broadcasted_iota(jnp.int32, (peers, rows), 0) == relative
    earlier = lax.broadcasted_iota(jnp.int32, (rows, rows), 0) < lax.broadcasted_iota(
        jnp.int32, (rows, rows), 1
    )
    counted = jnp.dot(
        jnp.where(hot, 1.0, 0.0).astype(jnp.bfloat16),
        jnp.where(earlier, 1.0, 0.0).astype(jnp.bfloat16),
        preferred_element_type=jnp.float32,
    )
    rank = jnp.sum(jnp.where(hot, counted, 0.0), axis=0, keepdims=True).astype(jnp.int32)
    slot = slot_ref[...]
    weight = counts_ref[...].astype(jnp.float32)
    line = lax.broadcasted_iota(jnp.int32, (8, rows), 0)
    facts = jnp.where(
        line == first % 8,
        (slot >> 8).astype(jnp.float32),
        jnp.where(
            line == first % 8 + 1,
            (slot & 255).astype(jnp.float32),
            jnp.where(line == first % 8 + 2, weight, 0.0),
        ),
    ).astype(jnp.bfloat16)
    places = lax.broadcasted_iota(jnp.int32, (columns, rows), 0)
    beyond = (lax.broadcasted_iota(jnp.int32, (8, columns), 0) == first % 8) & (
        lax.broadcasted_iota(jnp.int32, (8, columns), 1) >= capacity
    )
    for j in range(peers):
        match = places == jnp.where(relative == j, rank, -1)
        named = dot_rows(facts, jnp.where(match, 1.0, 0.0).astype(jnp.bfloat16))
        named = jnp.where(beyond, 255.0, named)
        scaled = jnp.where(match[:padded], weight, 0.0).astype(jnp.bfloat16)
        body = jnp.dot(scaled, vis_ref[...], preferred_element_type=jnp.float32)
        block = jnp.concatenate([body[: size - 8], body[size - 8 : size] + named], axis=0)
        out_ref = theirs_ref if j % 2 else mine_ref
        out_ref[j // 2] = block.astype(jnp.bfloat16)
    ahead.wait()


def dot_rows(left, right):
    return lax.dot_general(
        left, right, (((1,), (1,)), ((), ())), preferred_element_type=jnp.float32
    )


def groups(peers):
    chips = peers // 2
    return (
        [2 * k + 1 for k in range(chips)],
        [2 * k for k in range(chips) if k & (chips // 2)],
        [2 * k for k in range(chips) if not k & (chips // 2)],
    )


def load_kernel(peers, chunk, beam_ref, start_ref, after_ref, *refs):
    outs, buffer, sems = (refs[:3], refs[3:6], refs[6:9]), refs[9], refs[10]
    steps = beam_ref.shape[0] // chunk
    ahead = start_ref.shape[0] // chunk
    slots = buffer.shape[0]
    width = beam_ref.shape[1] // peers
    me = lax.axis_index("pair")

    def copy(step):
        return pltpu.make_async_copy(
            beam_ref.at[pl.ds(step * chunk, chunk)],
            buffer.at[step % slots],
            sems.at[step % slots],
        )

    for step in range(ahead, min(ahead + slots, steps)):
        copy(step).start()
    for step in range(steps):
        if step < ahead:
            source = start_ref.at[pl.ds(step * chunk, chunk)]
        else:
            copy(step).wait()
            source = buffer.at[step % slots]

        @pl.loop(0, chunk // 32)
        def _(line):
            at = pl.multiple_of(line * 32, 32)
            for (high_ref, again_ref, rest_ref), owners in zip(outs, groups(peers)):
                for i, j in enumerate(owners):
                    lane = pl.multiple_of((me ^ j) * width, width)
                    value = source[pl.ds(at, 32), pl.ds(lane, width)]
                    high = value.astype(jnp.bfloat16)
                    rest = value - high.astype(jnp.float32)
                    to = (pl.ds(step * chunk + at, 32), slice(i * width, (i + 1) * width))
                    high_ref[to] = high
                    again_ref[to] = (high * BEAM).astype(SMALL)
                    rest_ref[to] = (rest * BEAM_REST).astype(SMALL)

        if ahead <= step < steps - slots:
            copy(step + slots).start()


def stack_kernel(peers, capacity, mwin, *refs):
    pieces = refs[: peers // 2]
    held, (left_ref, small_ref, *send_refs) = refs[peers // 2 : -4], refs[-4:]
    first, size = block_rows(capacity)
    columns = pieces[0].shape[1]
    base_dev = left_ref.shape[2] // 2
    half = columns // (2 * mwin)
    tile = 512 if base_dev % 512 == 0 else base_dev
    rows, slots, weights = [], [], []
    for piece in pieces:
        values = piece[...].astype(jnp.float32)
        rows.append(values)
        for b in range(2):
            facts = values[(b + 1) * size - 8 : (b + 1) * size].T[:size]
            high = facts[:, first % 8 : first % 8 + 1]
            low = facts[:, first % 8 + 1 : first % 8 + 2]
            slots.append((high * 256.0 + low).astype(jnp.int32))
            weights.append(jnp.broadcast_to(facts[:, first % 8 + 2 : first % 8 + 3], (size, 128)))
    rows = jnp.concatenate(rows, axis=0).T
    weights = jnp.concatenate(weights, axis=0).T[:16]
    slots = jnp.concatenate(slots, axis=0)
    left = jnp.concatenate([rows, weights], axis=0).astype(jnp.bfloat16)
    places = lax.broadcasted_iota(jnp.int32, (slots.shape[0], tile), 1)
    for n in range(base_dev // tile):
        match = jnp.where(places == slots - n * tile, 1.0, 0.0).astype(jnp.bfloat16)
        sums = jnp.dot(left, match, preferred_element_type=jnp.float32)
        stacked = sums[:columns] * (1.0 / jnp.maximum(sums[columns : columns + 1], 1.0))
        high = stacked.astype(jnp.bfloat16)
        rest = (stacked - high.astype(jnp.float32)) * STACK_REST
        again = stacked * STACK
        straight = slice(n * tile, (n + 1) * tile)
        crossed = slice(base_dev + n * tile, base_dev + (n + 1) * tile)
        for m in range(mwin):
            at = 2 * half * m
            real, imag = slice(at, at + half), slice(at + half, at + 2 * half)
            upper, lower = slice(0, half), slice(half, 2 * half)
            for value, to in (
                (high, left_ref.at[m]),
                (rest, small_ref.at[m, 0]),
                (again, small_ref.at[m, 1]),
            ):
                to[upper, straight] = value[real].astype(to.dtype)
                to[lower, straight] = value[imag].astype(to.dtype)
                to[upper, crossed] = value[imag].astype(to.dtype)
                to[lower, crossed] = (-value[real]).astype(to.dtype)
    project(left_ref, small_ref, *held, *send_refs)


def project(left_ref, small_ref, high_ref, again_ref, rest_ref, *out_refs):
    mwin, half, depth = left_ref.shape
    width = out_refs[0].shape[2]
    for m in range(mwin):
        planes = slice(m * depth, (m + 1) * depth)
        rough = jnp.dot(left_ref[m], high_ref[planes], preferred_element_type=jnp.float32)
        fine = jnp.dot(
            small_ref[m, 0], again_ref[planes], preferred_element_type=jnp.float32
        ) + jnp.dot(small_ref[m, 1], rest_ref[planes], preferred_element_type=jnp.float32)
        total = rough + fine * (1.0 / (BEAM * STACK_REST))
        blocks = [out_ref.at[i] for out_ref in out_refs for i in range(out_ref.shape[0])]
        for i, block_ref in enumerate(blocks):
            block_ref[m * half : (m + 1) * half] = total[:, i * width : (i + 1) * width]


def keep_kernel(*refs):
    project(*refs[:5], refs[-1])


def staged(visibility, pair_counts, owner_ids, slot_ids, beam):
    peers = lax.axis_size("pair")
    chips = peers // 2
    rows, columns = visibility.shape[1:]
    capacity = 2 * rows // peers + 4
    mwin, _, base_dev, modes = beam.shape[1:]
    width = modes // peers
    _, size = block_rows(capacity)
    vmem = pl.BlockSpec(memory_space=pltpu.VMEM)
    anywhere = pl.BlockSpec(memory_space=pl.ANY)
    block = jax.ShapeDtypeStruct((chips, size, columns), jnp.bfloat16)
    facts = [value.reshape(1, rows) for value in (pair_counts, owner_ids, slot_ids)]
    chunk = 512
    planes = beam.reshape(mwin * 2 * base_dev, modes)
    mine, theirs, start = pl.pallas_call(
        functools.partial(pack_kernel, peers, capacity),
        out_shape=(block, block, pltpu.VMEM((AHEAD * chunk, modes), jnp.float32)),
        in_specs=[anywhere] * 5,
        out_specs=(vmem,) * 3,
        scratch_shapes=[pltpu.VMEM((rows, columns), jnp.bfloat16)]
        + [pltpu.VMEM((1, rows), jnp.int32)] * 3
        + [pltpu.SemaphoreType.DMA((5,))],
        compiler_params=pltpu.CompilerParams(vmem_limit_bytes=8 * MIB),
        name="pack",
    )(
        *[
            pltpu.with_memory_space_constraint(value, pltpu.HBM)
            for value in (visibility[0], *facts, planes)
        ]
    )
    got = swap(theirs, "pair", 1)
    pieces = [jnp.concatenate([mine[k], got[k]], axis=0) for k in range(chips)]
    order = [k for k in range(1, chips) if k & (chips // 2)] + [
        k for k in range(1, chips) if not k & (chips // 2)
    ]
    moved = {k: swap(pieces[k], "pair", 2 * k) for k in order}
    held = pl.pallas_call(
        functools.partial(load_kernel, peers, chunk),
        out_shape=tuple(
            pltpu.VMEM((planes.shape[0], len(owners) * width), dtype)
            for owners in groups(peers)
            for dtype in (jnp.bfloat16, SMALL, SMALL)
        ),
        in_specs=[anywhere, vmem, anywhere],
        out_specs=(vmem,) * 9,
        scratch_shapes=[
            pltpu.VMEM((4, chunk, modes), jnp.float32),
            pltpu.SemaphoreType.DMA((4,)),
        ],
        compiler_params=pltpu.CompilerParams(vmem_limit_bytes=12 * MIB),
        cost_estimate=pl.CostEstimate(
            flops=0, bytes_accessed=8 * planes.size, transcendentals=0
        ),
        name="load",
    )(planes, pltpu.with_memory_space_constraint(start, pltpu.VMEM), pieces[0])
    held = [pltpu.with_memory_space_constraint(part, pltpu.VMEM) for part in held]
    def products(count):
        return jax.ShapeDtypeStruct((count, columns, width), jnp.float32)

    def cost(count):
        flops = 6 * mwin * 2 * (columns // mwin) * base_dev * count * width
        return pl.CostEstimate(flops=flops, bytes_accessed=0, transcendentals=0)

    left, small, near_send, far_send = pl.pallas_call(
        functools.partial(stack_kernel, peers, capacity, mwin),
        out_shape=(
            pltpu.VMEM((mwin, columns // mwin, 2 * base_dev), jnp.bfloat16),
            pltpu.VMEM((mwin, 2, columns // mwin, 2 * base_dev), SMALL),
            products(chips // 2),
            products(chips // 2),
        ),
        in_specs=[vmem] * (chips + 3),
        out_specs=(vmem,) * 4,
        compiler_params=pltpu.CompilerParams(vmem_limit_bytes=12 * MIB),
        cost_estimate=cost(chips),
        name="stack",
    )(pieces[0], *[moved[k] for k in order], *held[:3])
    far_got, near_got = swap(far_send, "pair", 1), swap(near_send, "pair", 1)
    left, small = [pltpu.with_memory_space_constraint(part, pltpu.VMEM) for part in (left, small)]
    summed, after = {}, []
    for name, got, parts, owners in zip(
        ("far", "near"), (far_got, near_got), (held[3:6], held[6:9]), groups(peers)[1:]
    ):
        keep = pl.pallas_call(
            keep_kernel,
            out_shape=products(len(owners)),
            in_specs=[vmem] * 5 + [anywhere] * len(after),
            out_specs=vmem,
            compiler_params=pltpu.CompilerParams(vmem_limit_bytes=12 * MIB),
            cost_estimate=cost(len(owners)),
            name=name,
        )(left, small, *parts, *after)
        for i, j in enumerate(owners):
            k = j // 2
            summed[k] = keep[i] + got[i]
            if k:
                summed[k] = summed[k].astype(jnp.bfloat16)
            if k & (chips // 2):
                after.append(summed[k])
    amplitudes = summed[0]
    for k in order:
        if not k & (chips // 2):
            amplitudes = lax.optimization_barrier(amplitudes)
        partial = amplitudes
        last = swap(summed[k], "pair", 2 * k)
        amplitudes = partial + last.astype(jnp.float32)
    partial, last = lax.optimization_barrier((partial, last))
    modes_out = partial + last.astype(jnp.float32)
    sets = columns // (2 * mwin)
    power = jnp.sum((amplitudes * amplitudes).reshape(mwin, 2 * sets, width), axis=1)
    terms = [power] + [swap(power, "chan", d) for d in range(1, lax.axis_size("chan"))]
    while len(terms) > 1:
        terms = [one + other for one, other in zip(terms[::2], terms[1::2])]
    power = terms[0]
    power = power / (lax.axis_size("chan") * sets)
    shaped = modes_out.reshape(mwin, 2, sets, width).transpose(3, 0, 1, 2)
    return shaped[None], power.T


def plain(visibility, pair_counts, owner_ids, slot_ids, beam):
    peers = lax.axis_size("pair")
    pair_rows = pair_counts.shape[0]
    capacity = 2 * pair_rows // peers + 4
    owner = owner_ids[:, 0]
    order = jnp.argsort(owner, stable=True)
    sorted_owner = owner[order]
    owner_list = jnp.arange(peers, dtype=jnp.int32)
    first_at = jnp.searchsorted(sorted_owner, owner_list, side="left")
    last_at = jnp.searchsorted(sorted_owner, owner_list, side="right")
    ranks = jnp.arange(capacity, dtype=jnp.int32)
    valid = ranks[None, :] < (last_at - first_at)[:, None]
    where_at = jnp.clip(first_at[:, None] + ranks[None, :], 0, pair_rows - 1)
    picked = order[where_at]
    weights = jnp.where(valid, pair_counts[picked], 0)
    offsets = jnp.where(valid, slot_ids[picked], 0)
    rows = visibility[0][picked]
    weighted = (rows.astype(jnp.float32) * weights[:, :, None].astype(jnp.float32)).astype(
        jnp.bfloat16
    )
    got_rows, got_offsets, got_weights = (
        lax.all_to_all(weighted, "pair", split_axis=0, concat_axis=0, tiled=True),
        lax.all_to_all(offsets, "pair", split_axis=0, concat_axis=0, tiled=True),
        lax.all_to_all(weights, "pair", split_axis=0, concat_axis=0, tiled=True),
    )
    columns = got_rows.shape[2]
    got_rows = got_rows.reshape(peers * capacity, columns)
    got_offsets = got_offsets.reshape(peers * capacity)
    got_weights = got_weights.reshape(peers * capacity).astype(jnp.float32)
    beam_local = beam[0]
    mwin = beam_local.shape[0]
    base_dev = beam_local.shape[2]
    sets = columns // (2 * mwin)
    matches = jnp.arange(base_dev, dtype=jnp.int32)[:, None] == got_offsets[None, :]
    numer = jnp.dot(matches.astype(jnp.bfloat16), got_rows, preferred_element_type=jnp.float32)
    denom = jnp.sum(jnp.where(matches, got_weights[None, :], 0.0), axis=1)
    stacked = numer / jnp.maximum(denom, 1.0)[:, None]
    stacked = stacked.reshape(base_dev, mwin, 2 * sets)
    swapped = jnp.concatenate([stacked[:, :, sets:], -stacked[:, :, :sets]], axis=2)
    right = jnp.stack([stacked, swapped], axis=0)
    amplitudes = lax.psum_scatter(
        jnp.einsum(
            "mrbk,rbmc->kmc",
            beam_local,
            right,
            precision=lax.Precision.HIGHEST,
            preferred_element_type=jnp.float32,
        ),
        "pair",
        scatter_dimension=0,
        tiled=True,
    )
    power_local = jnp.sum(amplitudes * amplitudes, axis=2)
    total_power = lax.psum(power_local, "chan")
    mode_power = total_power / (lax.axis_size("chan") * sets)
    shaped = amplitudes.reshape(amplitudes.shape[0], mwin, 2, sets)
    return (shaped[None], mode_power)


def power_of_two(value):
    return value & (value - 1) == 0


def per_device(visibility, pair_counts, owner_ids, slot_ids, beam):
    peers, channels = lax.axis_size("pair"), lax.axis_size("chan")
    rows, columns = visibility.shape[1:]
    mwin, _, base_dev, modes = beam.shape[1:]
    capacity = 2 * rows // peers + 4
    fits = (
        1 < peers <= 8
        and power_of_two(peers)
        and power_of_two(channels)
        and rows % 128 == 0
        and columns % 128 == 0
        and capacity + 8 <= columns
        and base_dev % 512 == 0
        and modes % (128 * peers) == 0
        and columns % (32 * mwin) == 0
    )
    return (staged if fits else plain)(visibility, pair_counts, owner_ids, slot_ids, beam)


def solution(mesh):
    in_specs = (
        P("chan", "pair", None),
        P("pair"),
        P("pair", None),
        P("pair"),
        P("chan", None, None, "pair", None),
    )
    out_specs = (P("chan", "pair", None, None, None), P("pair", None))
    return jax.shard_map(
        per_device, mesh=mesh, in_specs=in_specs, out_specs=out_specs, check_vma=False
    )
```

```python
import functools

import jax
import jax.numpy as jnp
from jax import lax
from jax.experimental import pallas as pl
from jax.experimental.pallas import tpu as pltpu
from jax.sharding import PartitionSpec as P

MIB = 1 << 20
SMALL = jnp.float8_e5m2
AHEAD = 2
BEAM, BEAM_REST, STACK, STACK_REST = 2.0**18, 2.0**27, 2.0**12, 2.0**21


def round_up(value, unit):
    return -(-value // unit) * unit


def block_rows(capacity):
    first = capacity if capacity % 8 <= 5 else round_up(capacity, 8)
    return first, round_up(first + 3, 8)


def swap(value, axis, distance):
    size = lax.axis_size(axis)
    return lax.ppermute(value, axis, [(i, i ^ distance) for i in range(size)])


def pack_kernel(peers, capacity, *refs):
    sources, beam_ref, out_refs, start_ref = refs[:4], refs[4], refs[5 : 5 + peers // 2], refs[-6]
    held, sems = refs[-5:-1], refs[-1]
    copies = [
        pltpu.make_async_copy(source, target, sems.at[i])
        for i, (source, target) in enumerate(zip(sources, held))
    ]
    for copy in copies:
        copy.start()
    ahead = pltpu.make_async_copy(beam_ref.at[pl.ds(0, start_ref.shape[0])], start_ref, sems.at[4])
    ahead.start()
    for copy in copies:
        copy.wait()
    vis_ref, counts_ref, owner_ref, slot_ref = held
    rows, columns = vis_ref.shape
    first, size = block_rows(capacity)
    padded = round_up(size, 16)
    me = lax.axis_index("pair")
    relative = owner_ref[...] ^ me
    hot = lax.broadcasted_iota(jnp.int32, (peers, rows), 0) == relative
    earlier = lax.broadcasted_iota(jnp.int32, (rows, rows), 0) < lax.broadcasted_iota(
        jnp.int32, (rows, rows), 1
    )
    counted = jnp.dot(
        jnp.where(hot, 1.0, 0.0).astype(jnp.bfloat16),
        jnp.where(earlier, 1.0, 0.0).astype(jnp.bfloat16),
        preferred_element_type=jnp.float32,
    )
    rank = jnp.sum(jnp.where(hot, counted, 0.0), axis=0, keepdims=True).astype(jnp.int32)
    slot = slot_ref[...]
    weight = counts_ref[...].astype(jnp.float32)
    line = lax.broadcasted_iota(jnp.int32, (8, rows), 0)
    facts = jnp.where(
        line == first % 8,
        (slot >> 8).astype(jnp.float32),
        jnp.where(
            line == first % 8 + 1,
            (slot & 255).astype(jnp.float32),
            jnp.where(line == first % 8 + 2, weight, 0.0),
        ),
    ).astype(jnp.bfloat16)
    places = lax.broadcasted_iota(jnp.int32, (padded, rows), 0)
    beyond = (lax.broadcasted_iota(jnp.int32, (8, columns), 0) == first % 8) & (
        lax.broadcasted_iota(jnp.int32, (8, columns), 1) >= capacity
    )
    blocks = []
    for j in range(peers):
        match = places == jnp.where(relative == j, rank, -1)
        named = dot_rows(facts, jnp.where(match, 1.0, 0.0).astype(jnp.bfloat16))
        named = jnp.concatenate([named, jnp.zeros((8, columns - padded), jnp.float32)], axis=1)
        named = jnp.where(beyond, 255.0, named)
        scaled = jnp.where(match, weight, 0.0).astype(jnp.bfloat16)
        body = jnp.dot(scaled, vis_ref[...], preferred_element_type=jnp.float32)
        blocks += [body[: size - 8], body[size - 8 : size] + named]
        if j % 2:
            out_refs[j // 2][...] = jnp.concatenate(blocks, axis=0).astype(jnp.bfloat16)
            blocks = []
    ahead.wait()


def dot_rows(left, right):
    return lax.dot_general(
        left, right, (((1,), (1,)), ((), ())), preferred_element_type=jnp.float32
    )


def groups(peers):
    chips = peers // 2
    return (
        [2 * k + 1 for k in range(chips)],
        [2 * k for k in range(chips) if k & (chips // 2)],
        [2 * k for k in range(chips) if not k & (chips // 2)],
    )


def load_kernel(peers, chunk, beam_ref, start_ref, after_ref, *refs):
    outs, done_ref, buffer, sems = (refs[:3], refs[3:6], refs[6:9]), refs[9], refs[10], refs[11]
    done_ref[...] = jnp.zeros(done_ref.shape, done_ref.dtype)
    steps = beam_ref.shape[0] // chunk
    ahead = start_ref.shape[0] // chunk
    slots = buffer.shape[0]
    width = beam_ref.shape[1] // peers
    me = lax.axis_index("pair")

    def copy(step):
        return pltpu.make_async_copy(
            beam_ref.at[pl.ds(step * chunk, chunk)],
            buffer.at[step % slots],
            sems.at[step % slots],
        )

    for step in range(ahead, min(ahead + slots, steps)):
        copy(step).start()
    for step in range(steps):
        if step < ahead:
            source = start_ref.at[pl.ds(step * chunk, chunk)]
        else:
            copy(step).wait()
            source = buffer.at[step % slots]

        @pl.loop(0, chunk // 32)
        def _(line):
            at = pl.multiple_of(line * 32, 32)
            for (high_ref, again_ref, rest_ref), owners in zip(outs, groups(peers)):
                for i, j in enumerate(owners):
                    lane = pl.multiple_of((me ^ j) * width, width)
                    value = source[pl.ds(at, 32), pl.ds(lane, width)]
                    high = value.astype(jnp.bfloat16)
                    rest = value - high.astype(jnp.float32)
                    to = (pl.ds(step * chunk + at, 32), slice(i * width, (i + 1) * width))
                    high_ref[to] = high
                    again_ref[to] = (high * BEAM).astype(SMALL)
                    rest_ref[to] = (rest * BEAM_REST).astype(SMALL)

        if ahead <= step < steps - slots:
            copy(step + slots).start()


def add_up(capacity, blocks, base_dev, write):
    first, size = block_rows(capacity)
    slots, weights = [], []
    for block in blocks:
        facts = block[size - 8 :].T[:size]
        high = facts[:, first % 8 : first % 8 + 1]
        low = facts[:, first % 8 + 1 : first % 8 + 2]
        slots.append((high * 256.0 + low).astype(jnp.int32))
        weights.append(jnp.broadcast_to(facts[:, first % 8 + 2 : first % 8 + 3], (size, 128)))
    rows = jnp.concatenate(blocks, axis=0).T
    weights = jnp.concatenate(weights, axis=0).T[:16]
    slots = jnp.concatenate(slots, axis=0)
    left = jnp.concatenate([rows, weights], axis=0).astype(jnp.bfloat16)
    tile = 512
    places = lax.broadcasted_iota(jnp.int32, (slots.shape[0], tile), 1)
    for n in range(base_dev // tile):
        match = jnp.where(places == slots - n * tile, 1.0, 0.0).astype(jnp.bfloat16)
        write(n * tile, tile, jnp.dot(left, match, preferred_element_type=jnp.float32))


def pass_kernel(capacity, *refs):
    _, size = block_rows(capacity)
    blocks = [piece[...].astype(jnp.float32)[size:] for piece in refs[:-2]]
    refs[-1][...] = jnp.concatenate(blocks, axis=0).astype(jnp.bfloat16)


def direct_kernel(capacity, *refs):
    _, size = block_rows(capacity)
    sums_ref = refs[-1]

    def write(at, tile, sums):
        sums_ref[:, at : at + tile] = sums

    blocks = [piece[...].astype(jnp.float32)[:size] for piece in refs[:-2]]
    add_up(capacity, blocks, sums_ref.shape[1], write)


def stack_kernel(capacity, mwin, blocks_ref, direct_ref, *refs):
    held, (left_ref, small_ref, *send_refs) = refs[:3], refs[3:]
    _, size = block_rows(capacity)
    columns = blocks_ref.shape[1]
    base_dev = direct_ref.shape[1]
    half = columns // (2 * mwin)

    def write(at_n, tile, sums):
        sums = sums + direct_ref[:, at_n : at_n + tile]
        stacked = sums[:columns] * (1.0 / jnp.maximum(sums[columns : columns + 1], 1.0))
        high = stacked.astype(jnp.bfloat16)
        rest = (stacked - high.astype(jnp.float32)) * STACK_REST
        again = stacked * STACK
        straight = slice(at_n, at_n + tile)
        crossed = slice(base_dev + at_n, base_dev + at_n + tile)
        for m in range(mwin):
            at = 2 * half * m
            real, imag = slice(at, at + half), slice(at + half, at + 2 * half)
            upper, lower = slice(0, half), slice(half, 2 * half)
            for value, to in (
                (high, left_ref.at[m]),
                (rest, small_ref.at[m, 0]),
                (again, small_ref.at[m, 1]),
            ):
                to[upper, straight] = value[real].astype(to.dtype)
                to[lower, straight] = value[imag].astype(to.dtype)
                to[upper, crossed] = value[imag].astype(to.dtype)
                to[lower, crossed] = (-value[real]).astype(to.dtype)

    values = blocks_ref[...].astype(jnp.float32)
    blocks = [values[i : i + size] for i in range(0, values.shape[0], size)]
    add_up(capacity, blocks, base_dev, write)
    project(left_ref, small_ref, *held, *send_refs)


def project(left_ref, small_ref, high_ref, again_ref, rest_ref, *out_refs):
    mwin, half, depth = left_ref.shape
    width = out_refs[0].shape[2]
    for m in range(mwin):
        planes = slice(m * depth, (m + 1) * depth)
        rough = jnp.dot(left_ref[m], high_ref[planes], preferred_element_type=jnp.float32)
        fine = jnp.dot(
            small_ref[m, 0], again_ref[planes], preferred_element_type=jnp.float32
        ) + jnp.dot(small_ref[m, 1], rest_ref[planes], preferred_element_type=jnp.float32)
        total = rough + fine * (1.0 / (BEAM * STACK_REST))
        blocks = [out_ref.at[i] for out_ref in out_refs for i in range(out_ref.shape[0])]
        for i, block_ref in enumerate(blocks):
            block_ref[m * half : (m + 1) * half] = total[:, i * width : (i + 1) * width]


def keep_kernel(*refs):
    project(*refs[:5], refs[-1])


def staged(visibility, pair_counts, owner_ids, slot_ids, beam):
    peers = lax.axis_size("pair")
    chips = peers // 2
    rows, columns = visibility.shape[1:]
    capacity = 2 * rows // peers + 4
    mwin, _, base_dev, modes = beam.shape[1:]
    width = modes // peers
    _, size = block_rows(capacity)
    vmem = pl.BlockSpec(memory_space=pltpu.VMEM)
    anywhere = pl.BlockSpec(memory_space=pl.ANY)
    block = jax.ShapeDtypeStruct((2 * size, columns), jnp.bfloat16)
    facts = [value.reshape(1, rows) for value in (pair_counts, owner_ids, slot_ids)]
    chunk = 512
    planes = beam.reshape(mwin * 2 * base_dev, modes)
    *pieces, start = pl.pallas_call(
        functools.partial(pack_kernel, peers, capacity),
        out_shape=[block] * chips + [pltpu.VMEM((AHEAD * chunk, modes), jnp.float32)],
        in_specs=[anywhere] * 5,
        out_specs=[vmem] * (chips + 1),
        scratch_shapes=[pltpu.VMEM((rows, columns), jnp.bfloat16)]
        + [pltpu.VMEM((1, rows), jnp.int32)] * 3
        + [pltpu.SemaphoreType.DMA((5,))],
        compiler_params=pltpu.CompilerParams(vmem_limit_bytes=8 * MIB),
        name="pack",
    )(
        *[
            pltpu.with_memory_space_constraint(value, pltpu.HBM)
            for value in (visibility[0], *facts, planes)
        ]
    )
    order = [k for k in range(1, chips) if k & (chips // 2)] + [
        k for k in range(1, chips) if not k & (chips // 2)
    ]
    moved = {k: swap(pieces[k], "pair", 2 * k) for k in order}
    *held, loaded = pl.pallas_call(
        functools.partial(load_kernel, peers, chunk),
        out_shape=tuple(
            pltpu.VMEM((planes.shape[0], len(owners) * width), dtype)
            for owners in groups(peers)
            for dtype in (jnp.bfloat16, SMALL, SMALL)
        )
        + (jax.ShapeDtypeStruct((8, 128), jnp.float32),),
        in_specs=[anywhere, vmem, anywhere],
        out_specs=(vmem,) * 10,
        scratch_shapes=[
            pltpu.VMEM((4, chunk, modes), jnp.float32),
            pltpu.SemaphoreType.DMA((4,)),
        ],
        compiler_params=pltpu.CompilerParams(vmem_limit_bytes=12 * MIB),
        cost_estimate=pl.CostEstimate(
            flops=0, bytes_accessed=8 * planes.size, transcendentals=0
        ),
        name="load",
    )(planes, pltpu.with_memory_space_constraint(start, pltpu.VMEM), pieces[0])
    held = [pltpu.with_memory_space_constraint(part, pltpu.VMEM) for part in held]

    def products(count):
        return jax.ShapeDtypeStruct((count, columns, width), jnp.float32)

    def cost(count):
        flops = 6 * mwin * 2 * (columns // mwin) * base_dev * count * width
        return pl.CostEstimate(flops=flops, bytes_accessed=0, transcendentals=0)

    received = [pieces[0]] + [moved[k] for k in order]
    passed = pl.pallas_call(
        functools.partial(pass_kernel, capacity),
        out_shape=jax.ShapeDtypeStruct((chips * size, columns), jnp.bfloat16),
        in_specs=[vmem] * chips + [anywhere],
        out_specs=vmem,
        compiler_params=pltpu.CompilerParams(vmem_limit_bytes=8 * MIB),
        name="pass",
    )(*received, loaded)
    got = swap(passed, "pair", 1)
    direct = pl.pallas_call(
        functools.partial(direct_kernel, capacity),
        out_shape=pltpu.VMEM((columns + 16, base_dev), jnp.float32),
        in_specs=[vmem] * chips + [anywhere],
        out_specs=vmem,
        compiler_params=pltpu.CompilerParams(vmem_limit_bytes=12 * MIB),
        cost_estimate=cost(1),
        name="direct",
    )(*received, loaded)
    left, small, near_send, far_send = pl.pallas_call(
        functools.partial(stack_kernel, capacity, mwin),
        out_shape=(
            pltpu.VMEM((mwin, columns // mwin, 2 * base_dev), jnp.bfloat16),
            pltpu.VMEM((mwin, 2, columns // mwin, 2 * base_dev), SMALL),
            products(chips // 2),
            products(chips // 2),
        ),
        in_specs=[vmem] * 5,
        out_specs=(vmem,) * 4,
        compiler_params=pltpu.CompilerParams(vmem_limit_bytes=12 * MIB),
        cost_estimate=cost(chips),
        name="stack",
    )(got, pltpu.with_memory_space_constraint(direct, pltpu.VMEM), *held[:3])
    far_got, near_got = swap(far_send, "pair", 1), swap(near_send, "pair", 1)
    left, small = [pltpu.with_memory_space_constraint(part, pltpu.VMEM) for part in (left, small)]
    summed, after = {}, []
    for name, got, parts, owners in zip(
        ("far", "near"), (far_got, near_got), (held[3:6], held[6:9]), groups(peers)[1:]
    ):
        keep = pl.pallas_call(
            keep_kernel,
            out_shape=products(len(owners)),
            in_specs=[vmem] * 5 + [anywhere] * len(after),
            out_specs=vmem,
            compiler_params=pltpu.CompilerParams(vmem_limit_bytes=12 * MIB),
            cost_estimate=cost(len(owners)),
            name=name,
        )(left, small, *parts, *after)
        for i, j in enumerate(owners):
            k = j // 2
            summed[k] = keep[i] + got[i]
            if k:
                summed[k] = summed[k].astype(jnp.bfloat16)
            if k & (chips // 2):
                after.append(summed[k])
    amplitudes = summed[0]
    for k in order:
        if not k & (chips // 2):
            amplitudes = lax.optimization_barrier(amplitudes)
        partial = amplitudes
        last = swap(summed[k], "pair", 2 * k)
        amplitudes = partial + last.astype(jnp.float32)
    partial, last = lax.optimization_barrier((partial, last))
    modes_out = partial + last.astype(jnp.float32)
    sets = columns // (2 * mwin)
    power = jnp.sum((amplitudes * amplitudes).reshape(mwin, 2 * sets, width), axis=1)
    terms = [power] + [swap(power, "chan", d) for d in range(1, lax.axis_size("chan"))]
    while len(terms) > 1:
        terms = [one + other for one, other in zip(terms[::2], terms[1::2])]
    power = terms[0]
    power = power / (lax.axis_size("chan") * sets)
    shaped = modes_out.reshape(mwin, 2, sets, width).transpose(3, 0, 1, 2)
    return shaped[None], power.T


def plain(visibility, pair_counts, owner_ids, slot_ids, beam):
    peers = lax.axis_size("pair")
    pair_rows = pair_counts.shape[0]
    capacity = 2 * pair_rows // peers + 4
    owner = owner_ids[:, 0]
    order = jnp.argsort(owner, stable=True)
    sorted_owner = owner[order]
    owner_list = jnp.arange(peers, dtype=jnp.int32)
    first_at = jnp.searchsorted(sorted_owner, owner_list, side="left")
    last_at = jnp.searchsorted(sorted_owner, owner_list, side="right")
    ranks = jnp.arange(capacity, dtype=jnp.int32)
    valid = ranks[None, :] < (last_at - first_at)[:, None]
    where_at = jnp.clip(first_at[:, None] + ranks[None, :], 0, pair_rows - 1)
    picked = order[where_at]
    weights = jnp.where(valid, pair_counts[picked], 0)
    offsets = jnp.where(valid, slot_ids[picked], 0)
    rows = visibility[0][picked]
    weighted = (rows.astype(jnp.float32) * weights[:, :, None].astype(jnp.float32)).astype(
        jnp.bfloat16
    )
    got_rows, got_offsets, got_weights = (
        lax.all_to_all(weighted, "pair", split_axis=0, concat_axis=0, tiled=True),
        lax.all_to_all(offsets, "pair", split_axis=0, concat_axis=0, tiled=True),
        lax.all_to_all(weights, "pair", split_axis=0, concat_axis=0, tiled=True),
    )
    columns = got_rows.shape[2]
    got_rows = got_rows.reshape(peers * capacity, columns)
    got_offsets = got_offsets.reshape(peers * capacity)
    got_weights = got_weights.reshape(peers * capacity).astype(jnp.float32)
    beam_local = beam[0]
    mwin = beam_local.shape[0]
    base_dev = beam_local.shape[2]
    sets = columns // (2 * mwin)
    matches = jnp.arange(base_dev, dtype=jnp.int32)[:, None] == got_offsets[None, :]
    numer = jnp.dot(matches.astype(jnp.bfloat16), got_rows, preferred_element_type=jnp.float32)
    denom = jnp.sum(jnp.where(matches, got_weights[None, :], 0.0), axis=1)
    stacked = numer / jnp.maximum(denom, 1.0)[:, None]
    stacked = stacked.reshape(base_dev, mwin, 2 * sets)
    swapped = jnp.concatenate([stacked[:, :, sets:], -stacked[:, :, :sets]], axis=2)
    right = jnp.stack([stacked, swapped], axis=0)
    amplitudes = lax.psum_scatter(
        jnp.einsum(
            "mrbk,rbmc->kmc",
            beam_local,
            right,
            precision=lax.Precision.HIGHEST,
            preferred_element_type=jnp.float32,
        ),
        "pair",
        scatter_dimension=0,
        tiled=True,
    )
    power_local = jnp.sum(amplitudes * amplitudes, axis=2)
    total_power = lax.psum(power_local, "chan")
    mode_power = total_power / (lax.axis_size("chan") * sets)
    shaped = amplitudes.reshape(amplitudes.shape[0], mwin, 2, sets)
    return (shaped[None], mode_power)


def power_of_two(value):
    return value & (value - 1) == 0


def per_device(visibility, pair_counts, owner_ids, slot_ids, beam):
    peers, channels = lax.axis_size("pair"), lax.axis_size("chan")
    rows, columns = visibility.shape[1:]
    mwin, _, base_dev, modes = beam.shape[1:]
    capacity = 2 * rows // peers + 4
    fits = (
        1 < peers <= 8
        and power_of_two(peers)
        and power_of_two(channels)
        and rows % 128 == 0
        and columns % 128 == 0
        and capacity + 8 <= columns
        and base_dev % 512 == 0
        and modes % (128 * peers) == 0
        and columns % (32 * mwin) == 0
    )
    return (staged if fits else plain)(visibility, pair_counts, owner_ids, slot_ids, beam)


def solution(mesh):
    in_specs = (
        P("chan", "pair", None),
        P("pair"),
        P("pair", None),
        P("pair"),
        P("chan", None, None, "pair", None),
    )
    out_specs = (P("chan", "pair", None, None, None), P("pair", None))
    return jax.shard_map(
        per_device, mesh=mesh, in_specs=in_specs, out_specs=out_specs, check_vma=False
    )
```

```python
import functools

import jax
import jax.numpy as jnp
from jax import lax
from jax.experimental import pallas as pl
from jax.experimental.pallas import tpu as pltpu
from jax.sharding import PartitionSpec as P

MIB = 1 << 20
SMALL = jnp.float8_e5m2
AHEAD = 4
BEAM, BEAM_REST, STACK, STACK_REST = 2.0**18, 2.0**27, 2.0**12, 2.0**21


def round_up(value, unit):
    return -(-value // unit) * unit


def block_rows(capacity):
    first = capacity if capacity % 8 <= 5 else round_up(capacity, 8)
    return first, round_up(first + 3, 8)


def swap(value, axis, distance):
    size = lax.axis_size(axis)
    return lax.ppermute(value, axis, [(i, i ^ distance) for i in range(size)])


def pack_kernel(peers, capacity, *refs):
    sources, beam_ref, out_refs, start_ref = refs[:4], refs[4], refs[5 : 5 + peers // 2], refs[-6]
    held, sems = refs[-5:-1], refs[-1]
    copies = [
        pltpu.make_async_copy(source, target, sems.at[i])
        for i, (source, target) in enumerate(zip(sources, held))
    ]
    for copy in copies:
        copy.start()
    ahead = pltpu.make_async_copy(beam_ref.at[pl.ds(0, start_ref.shape[0])], start_ref, sems.at[4])
    ahead.start()
    for copy in copies:
        copy.wait()
    vis_ref, counts_ref, owner_ref, slot_ref = held
    rows, columns = vis_ref.shape
    first, size = block_rows(capacity)
    padded = round_up(size, 16)
    me = lax.axis_index("pair")
    relative = owner_ref[...] ^ me
    hot = lax.broadcasted_iota(jnp.int32, (peers, rows), 0) == relative
    earlier = lax.broadcasted_iota(jnp.int32, (rows, rows), 0) < lax.broadcasted_iota(
        jnp.int32, (rows, rows), 1
    )
    counted = jnp.dot(
        jnp.where(hot, 1.0, 0.0).astype(jnp.bfloat16),
        jnp.where(earlier, 1.0, 0.0).astype(jnp.bfloat16),
        preferred_element_type=jnp.float32,
    )
    rank = jnp.sum(jnp.where(hot, counted, 0.0), axis=0, keepdims=True).astype(jnp.int32)
    slot = slot_ref[...]
    weight = counts_ref[...].astype(jnp.float32)
    line = lax.broadcasted_iota(jnp.int32, (8, rows), 0)
    facts = jnp.where(
        line == first % 8,
        (slot >> 8).astype(jnp.float32),
        jnp.where(
            line == first % 8 + 1,
            (slot & 255).astype(jnp.float32),
            jnp.where(line == first % 8 + 2, weight, 0.0),
        ),
    ).astype(jnp.bfloat16)
    places = lax.broadcasted_iota(jnp.int32, (padded, rows), 0)
    beyond = (lax.broadcasted_iota(jnp.int32, (8, columns), 0) == first % 8) & (
        lax.broadcasted_iota(jnp.int32, (8, columns), 1) >= capacity
    )
    blocks = []
    for j in range(peers):
        match = places == jnp.where(relative == j, rank, -1)
        named = dot_rows(facts, jnp.where(match, 1.0, 0.0).astype(jnp.bfloat16))
        named = jnp.concatenate([named, jnp.zeros((8, columns - padded), jnp.float32)], axis=1)
        named = jnp.where(beyond, 255.0, named)
        scaled = jnp.where(match, weight, 0.0).astype(jnp.bfloat16)
        body = jnp.dot(scaled, vis_ref[...], preferred_element_type=jnp.float32)
        blocks += [body[: size - 8], body[size - 8 : size] + named]
        if j % 2:
            out_refs[j // 2][...] = jnp.concatenate(blocks, axis=0).astype(jnp.bfloat16)
            blocks = []
    ahead.wait()


def dot_rows(left, right):
    return lax.dot_general(
        left, right, (((1,), (1,)), ((), ())), preferred_element_type=jnp.float32
    )


def groups(peers):
    chips = peers // 2
    return (
        [2 * k + 1 for k in range(chips)],
        [2 * k for k in range(chips) if k & (chips // 2)],
        [2 * k for k in range(chips) if not k & (chips // 2)],
    )


def load_kernel(peers, chunk, beam_ref, start_ref, after_ref, *refs):
    outs, done_ref, buffer, sems = (refs[:3], refs[3:6], refs[6:9]), refs[9], refs[10], refs[11]
    done_ref[...] = jnp.zeros(done_ref.shape, done_ref.dtype)
    steps = beam_ref.shape[0] // chunk
    ahead = start_ref.shape[0] // chunk
    slots = buffer.shape[0]
    width = beam_ref.shape[1] // peers
    me = lax.axis_index("pair")

    def copy(step):
        return pltpu.make_async_copy(
            beam_ref.at[pl.ds(step * chunk, chunk)],
            buffer.at[step % slots],
            sems.at[step % slots],
        )

    for step in range(ahead, min(ahead + slots, steps)):
        copy(step).start()
    for step in range(steps):
        if step < ahead:
            source = start_ref.at[pl.ds(step * chunk, chunk)]
        else:
            copy(step).wait()
            source = buffer.at[step % slots]

        @pl.loop(0, chunk // 32)
        def _(line):
            at = pl.multiple_of(line * 32, 32)
            for (high_ref, again_ref, rest_ref), owners in zip(outs, groups(peers)):
                for i, j in enumerate(owners):
                    lane = pl.multiple_of((me ^ j) * width, width)
                    value = source[pl.ds(at, 32), pl.ds(lane, width)]
                    high = value.astype(jnp.bfloat16)
                    rest = value - high.astype(jnp.float32)
                    to = (pl.ds(step * chunk + at, 32), slice(i * width, (i + 1) * width))
                    high_ref[to] = high
                    again_ref[to] = (high * BEAM).astype(SMALL)
                    rest_ref[to] = (rest * BEAM_REST).astype(SMALL)

        if ahead <= step < steps - slots:
            copy(step + slots).start()


def add_up(capacity, blocks, base_dev, write):
    first, size = block_rows(capacity)
    slots, weights = [], []
    for block in blocks:
        facts = block[size - 8 :].T[:size]
        high = facts[:, first % 8 : first % 8 + 1]
        low = facts[:, first % 8 + 1 : first % 8 + 2]
        slots.append((high * 256.0 + low).astype(jnp.int32))
        weights.append(jnp.broadcast_to(facts[:, first % 8 + 2 : first % 8 + 3], (size, 128)))
    rows = jnp.concatenate(blocks, axis=0).T
    weights = jnp.concatenate(weights, axis=0).T[:16]
    slots = jnp.concatenate(slots, axis=0)
    left = jnp.concatenate([rows, weights], axis=0).astype(jnp.bfloat16)
    tile = 512
    places = lax.broadcasted_iota(jnp.int32, (slots.shape[0], tile), 1)
    for n in range(base_dev // tile):
        match = jnp.where(places == slots - n * tile, 1.0, 0.0).astype(jnp.bfloat16)
        write(n * tile, tile, jnp.dot(left, match, preferred_element_type=jnp.float32))


def pass_kernel(capacity, *refs):
    _, size = block_rows(capacity)
    blocks = [piece[...].astype(jnp.float32)[size:] for piece in refs[:-2]]
    refs[-1][...] = jnp.concatenate(blocks, axis=0).astype(jnp.bfloat16)


def direct_kernel(capacity, *refs):
    _, size = block_rows(capacity)
    sums_ref = refs[-1]

    def write(at, tile, sums):
        sums_ref[:, at : at + tile] = sums

    blocks = [piece[...].astype(jnp.float32)[:size] for piece in refs[:-2]]
    add_up(capacity, blocks, sums_ref.shape[1], write)


def stack_kernel(capacity, mwin, blocks_ref, direct_ref, *refs):
    held, (left_ref, small_ref, *send_refs) = refs[:3], refs[3:]
    _, size = block_rows(capacity)
    columns = blocks_ref.shape[1]
    base_dev = direct_ref.shape[1]
    half = columns // (2 * mwin)

    def write(at_n, tile, sums):
        sums = sums + direct_ref[:, at_n : at_n + tile]
        stacked = sums[:columns] * (1.0 / jnp.maximum(sums[columns : columns + 1], 1.0))
        high = stacked.astype(jnp.bfloat16)
        rest = (stacked - high.astype(jnp.float32)) * STACK_REST
        again = stacked * STACK
        straight = slice(at_n, at_n + tile)
        crossed = slice(base_dev + at_n, base_dev + at_n + tile)
        for m in range(mwin):
            at = 2 * half * m
            real, imag = slice(at, at + half), slice(at + half, at + 2 * half)
            upper, lower = slice(0, half), slice(half, 2 * half)
            for value, to in (
                (high, left_ref.at[m]),
                (rest, small_ref.at[m, 0]),
                (again, small_ref.at[m, 1]),
            ):
                to[upper, straight] = value[real].astype(to.dtype)
                to[lower, straight] = value[imag].astype(to.dtype)
                to[upper, crossed] = value[imag].astype(to.dtype)
                to[lower, crossed] = (-value[real]).astype(to.dtype)

    values = blocks_ref[...].astype(jnp.float32)
    blocks = [values[i : i + size] for i in range(0, values.shape[0], size)]
    add_up(capacity, blocks, base_dev, write)
    project(left_ref, small_ref, *held, *send_refs)


def project(left_ref, small_ref, high_ref, again_ref, rest_ref, *out_refs):
    mwin, half, depth = left_ref.shape
    width = out_refs[0].shape[2]
    for m in range(mwin):
        planes = slice(m * depth, (m + 1) * depth)
        rough = jnp.dot(left_ref[m], high_ref[planes], preferred_element_type=jnp.float32)
        fine = jnp.dot(
            small_ref[m, 0], again_ref[planes], preferred_element_type=jnp.float32
        ) + jnp.dot(small_ref[m, 1], rest_ref[planes], preferred_element_type=jnp.float32)
        total = rough + fine * (1.0 / (BEAM * STACK_REST))
        blocks = [out_ref.at[i] for out_ref in out_refs for i in range(out_ref.shape[0])]
        for i, block_ref in enumerate(blocks):
            block_ref[m * half : (m + 1) * half] = total[:, i * width : (i + 1) * width]


def keep_kernel(*refs):
    project(*refs[:5], refs[-1])


def staged(visibility, pair_counts, owner_ids, slot_ids, beam):
    peers = lax.axis_size("pair")
    chips = peers // 2
    rows, columns = visibility.shape[1:]
    capacity = 2 * rows // peers + 4
    mwin, _, base_dev, modes = beam.shape[1:]
    width = modes // peers
    _, size = block_rows(capacity)
    vmem = pl.BlockSpec(memory_space=pltpu.VMEM)
    anywhere = pl.BlockSpec(memory_space=pl.ANY)
    block = jax.ShapeDtypeStruct((2 * size, columns), jnp.bfloat16)
    facts = [value.reshape(1, rows) for value in (pair_counts, owner_ids, slot_ids)]
    chunk = 128
    planes = beam.reshape(mwin * 2 * base_dev, modes)
    *pieces, start = pl.pallas_call(
        functools.partial(pack_kernel, peers, capacity),
        out_shape=[block] * chips + [pltpu.VMEM((AHEAD * chunk, modes), jnp.float32)],
        in_specs=[anywhere] * 5,
        out_specs=[vmem] * (chips + 1),
        scratch_shapes=[pltpu.VMEM((rows, columns), jnp.bfloat16)]
        + [pltpu.VMEM((1, rows), jnp.int32)] * 3
        + [pltpu.SemaphoreType.DMA((5,))],
        compiler_params=pltpu.CompilerParams(vmem_limit_bytes=8 * MIB),
        name="pack",
    )(
        *[
            pltpu.with_memory_space_constraint(value, pltpu.HBM)
            for value in (visibility[0], *facts, planes)
        ]
    )
    order = [k for k in range(1, chips) if k & (chips // 2)] + [
        k for k in range(1, chips) if not k & (chips // 2)
    ]
    moved = {k: swap(pieces[k], "pair", 2 * k) for k in order}
    *held, loaded = pl.pallas_call(
        functools.partial(load_kernel, peers, chunk),
        out_shape=tuple(
            pltpu.VMEM((planes.shape[0], len(owners) * width), dtype)
            for owners in groups(peers)
            for dtype in (jnp.bfloat16, SMALL, SMALL)
        )
        + (jax.ShapeDtypeStruct((8, 128), jnp.float32),),
        in_specs=[anywhere, vmem, anywhere],
        out_specs=(vmem,) * 10,
        scratch_shapes=[
            pltpu.VMEM((16, chunk, modes), jnp.float32),
            pltpu.SemaphoreType.DMA((16,)),
        ],
        compiler_params=pltpu.CompilerParams(vmem_limit_bytes=12 * MIB),
        cost_estimate=pl.CostEstimate(
            flops=0, bytes_accessed=8 * planes.size, transcendentals=0
        ),
        name="load",
    )(planes, pltpu.with_memory_space_constraint(start, pltpu.VMEM), pieces[0])
    held = [pltpu.with_memory_space_constraint(part, pltpu.VMEM) for part in held]

    def products(count):
        return jax.ShapeDtypeStruct((count, columns, width), jnp.float32)

    def cost(count):
        flops = 6 * mwin * 2 * (columns // mwin) * base_dev * count * width
        return pl.CostEstimate(flops=flops, bytes_accessed=0, transcendentals=0)

    received = [pieces[0]] + [moved[k] for k in order]
    passed = pl.pallas_call(
        functools.partial(pass_kernel, capacity),
        out_shape=jax.ShapeDtypeStruct((chips * size, columns), jnp.bfloat16),
        in_specs=[vmem] * chips + [anywhere],
        out_specs=vmem,
        compiler_params=pltpu.CompilerParams(vmem_limit_bytes=8 * MIB),
        name="pass",
    )(*received, loaded)
    got = swap(passed, "pair", 1)
    direct = pl.pallas_call(
        functools.partial(direct_kernel, capacity),
        out_shape=pltpu.VMEM((columns + 16, base_dev), jnp.float32),
        in_specs=[vmem] * chips + [anywhere],
        out_specs=vmem,
        compiler_params=pltpu.CompilerParams(vmem_limit_bytes=12 * MIB),
        cost_estimate=cost(1),
        name="direct",
    )(*received, loaded)
    left, small, near_send, far_send = pl.pallas_call(
        functools.partial(stack_kernel, capacity, mwin),
        out_shape=(
            pltpu.VMEM((mwin, columns // mwin, 2 * base_dev), jnp.bfloat16),
            pltpu.VMEM((mwin, 2, columns // mwin, 2 * base_dev), SMALL),
            products(chips // 2),
            products(chips // 2),
        ),
        in_specs=[vmem] * 5,
        out_specs=(vmem,) * 4,
        compiler_params=pltpu.CompilerParams(vmem_limit_bytes=12 * MIB),
        cost_estimate=cost(chips),
        name="stack",
    )(got, pltpu.with_memory_space_constraint(direct, pltpu.VMEM), *held[:3])
    far_got, near_got = swap(far_send, "pair", 1), swap(near_send, "pair", 1)
    left, small = [pltpu.with_memory_space_constraint(part, pltpu.VMEM) for part in (left, small)]
    summed, after = {}, []
    for name, got, parts, owners in zip(
        ("far", "near"), (far_got, near_got), (held[3:6], held[6:9]), groups(peers)[1:]
    ):
        keep = pl.pallas_call(
            keep_kernel,
            out_shape=products(len(owners)),
            in_specs=[vmem] * 5 + [anywhere] * len(after),
            out_specs=vmem,
            compiler_params=pltpu.CompilerParams(vmem_limit_bytes=12 * MIB),
            cost_estimate=cost(len(owners)),
            name=name,
        )(left, small, *parts, *after)
        for i, j in enumerate(owners):
            k = j // 2
            summed[k] = keep[i] + got[i]
            if k:
                summed[k] = summed[k].astype(jnp.bfloat16)
            if k & (chips // 2):
                after.append(summed[k])
    amplitudes = summed[0]
    for k in order:
        if not k & (chips // 2):
            amplitudes = lax.optimization_barrier(amplitudes)
        partial = amplitudes
        last = swap(summed[k], "pair", 2 * k)
        amplitudes = partial + last.astype(jnp.float32)
    partial, last = lax.optimization_barrier((partial, last))
    modes_out = partial + last.astype(jnp.float32)
    sets = columns // (2 * mwin)
    power = jnp.sum((amplitudes * amplitudes).reshape(mwin, 2 * sets, width), axis=1)
    terms = [power] + [swap(power, "chan", d) for d in range(1, lax.axis_size("chan"))]
    while len(terms) > 1:
        terms = [one + other for one, other in zip(terms[::2], terms[1::2])]
    power = terms[0]
    power = power / (lax.axis_size("chan") * sets)
    shaped = modes_out.reshape(mwin, 2, sets, width).transpose(3, 0, 1, 2)
    return shaped[None], power.T


def plain(visibility, pair_counts, owner_ids, slot_ids, beam):
    peers = lax.axis_size("pair")
    pair_rows = pair_counts.shape[0]
    capacity = 2 * pair_rows // peers + 4
    owner = owner_ids[:, 0]
    order = jnp.argsort(owner, stable=True)
    sorted_owner = owner[order]
    owner_list = jnp.arange(peers, dtype=jnp.int32)
    first_at = jnp.searchsorted(sorted_owner, owner_list, side="left")
    last_at = jnp.searchsorted(sorted_owner, owner_list, side="right")
    ranks = jnp.arange(capacity, dtype=jnp.int32)
    valid = ranks[None, :] < (last_at - first_at)[:, None]
    where_at = jnp.clip(first_at[:, None] + ranks[None, :], 0, pair_rows - 1)
    picked = order[where_at]
    weights = jnp.where(valid, pair_counts[picked], 0)
    offsets = jnp.where(valid, slot_ids[picked], 0)
    rows = visibility[0][picked]
    weighted = (rows.astype(jnp.float32) * weights[:, :, None].astype(jnp.float32)).astype(
        jnp.bfloat16
    )
    got_rows, got_offsets, got_weights = (
        lax.all_to_all(weighted, "pair", split_axis=0, concat_axis=0, tiled=True),
        lax.all_to_all(offsets, "pair", split_axis=0, concat_axis=0, tiled=True),
        lax.all_to_all(weights, "pair", split_axis=0, concat_axis=0, tiled=True),
    )
    columns = got_rows.shape[2]
    got_rows = got_rows.reshape(peers * capacity, columns)
    got_offsets = got_offsets.reshape(peers * capacity)
    got_weights = got_weights.reshape(peers * capacity).astype(jnp.float32)
    beam_local = beam[0]
    mwin = beam_local.shape[0]
    base_dev = beam_local.shape[2]
    sets = columns // (2 * mwin)
    matches = jnp.arange(base_dev, dtype=jnp.int32)[:, None] == got_offsets[None, :]
    numer = jnp.dot(matches.astype(jnp.bfloat16), got_rows, preferred_element_type=jnp.float32)
    denom = jnp.sum(jnp.where(matches, got_weights[None, :], 0.0), axis=1)
    stacked = numer / jnp.maximum(denom, 1.0)[:, None]
    stacked = stacked.reshape(base_dev, mwin, 2 * sets)
    swapped = jnp.concatenate([stacked[:, :, sets:], -stacked[:, :, :sets]], axis=2)
    right = jnp.stack([stacked, swapped], axis=0)
    amplitudes = lax.psum_scatter(
        jnp.einsum(
            "mrbk,rbmc->kmc",
            beam_local,
            right,
            precision=lax.Precision.HIGHEST,
            preferred_element_type=jnp.float32,
        ),
        "pair",
        scatter_dimension=0,
        tiled=True,
    )
    power_local = jnp.sum(amplitudes * amplitudes, axis=2)
    total_power = lax.psum(power_local, "chan")
    mode_power = total_power / (lax.axis_size("chan") * sets)
    shaped = amplitudes.reshape(amplitudes.shape[0], mwin, 2, sets)
    return (shaped[None], mode_power)


def power_of_two(value):
    return value & (value - 1) == 0


def per_device(visibility, pair_counts, owner_ids, slot_ids, beam):
    peers, channels = lax.axis_size("pair"), lax.axis_size("chan")
    rows, columns = visibility.shape[1:]
    mwin, _, base_dev, modes = beam.shape[1:]
    capacity = 2 * rows // peers + 4
    fits = (
        1 < peers <= 8
        and power_of_two(peers)
        and power_of_two(channels)
        and rows % 128 == 0
        and columns % 128 == 0
        and capacity + 8 <= columns
        and base_dev % 512 == 0
        and modes % (128 * peers) == 0
        and columns % (32 * mwin) == 0
    )
    return (staged if fits else plain)(visibility, pair_counts, owner_ids, slot_ids, beam)


def solution(mesh):
    in_specs = (
        P("chan", "pair", None),
        P("pair"),
        P("pair", None),
        P("pair"),
        P("chan", None, None, "pair", None),
    )
    out_specs = (P("chan", "pair", None, None, None), P("pair", None))
    return jax.shard_map(
        per_device, mesh=mesh, in_specs=in_specs, out_specs=out_specs, check_vma=False
    )
```

```python
import functools

import jax
import jax.numpy as jnp
from jax import lax
from jax.experimental import pallas as pl
from jax.experimental.pallas import tpu as pltpu
from jax.sharding import PartitionSpec as P

MIB = 1 << 20
SMALL = jnp.float8_e5m2
AHEAD = 4
BEAM, BEAM_REST, STACK, STACK_REST = 2.0**18, 2.0**27, 2.0**12, 2.0**21


def round_up(value, unit):
    return -(-value // unit) * unit


def block_rows(capacity):
    first = capacity if capacity % 8 <= 5 else round_up(capacity, 8)
    return first, round_up(first + 3, 8)


def swap(value, axis, distance):
    size = lax.axis_size(axis)
    return lax.ppermute(value, axis, [(i, i ^ distance) for i in range(size)])


def pack_kernel(peers, capacity, *refs):
    sources, beam_ref, out_refs, start_ref = refs[:4], refs[4], refs[5 : 5 + peers // 2], refs[-6]
    held, sems = refs[-5:-1], refs[-1]
    copies = [
        pltpu.make_async_copy(source, target, sems.at[i])
        for i, (source, target) in enumerate(zip(sources, held))
    ]
    for copy in copies:
        copy.start()
    ahead = pltpu.make_async_copy(beam_ref.at[pl.ds(0, start_ref.shape[0])], start_ref, sems.at[4])
    ahead.start()
    for copy in copies:
        copy.wait()
    vis_ref, counts_ref, owner_ref, slot_ref = held
    rows, columns = vis_ref.shape
    first, size = block_rows(capacity)
    padded = round_up(size, 16)
    me = lax.axis_index("pair")
    relative = owner_ref[...] ^ me
    hot = lax.broadcasted_iota(jnp.int32, (peers, rows), 0) == relative
    earlier = lax.broadcasted_iota(jnp.int32, (rows, rows), 0) < lax.broadcasted_iota(
        jnp.int32, (rows, rows), 1
    )
    counted = jnp.dot(
        jnp.where(hot, 1.0, 0.0).astype(jnp.bfloat16),
        jnp.where(earlier, 1.0, 0.0).astype(jnp.bfloat16),
        preferred_element_type=jnp.float32,
    )
    rank = jnp.sum(jnp.where(hot, counted, 0.0), axis=0, keepdims=True).astype(jnp.int32)
    slot = slot_ref[...]
    weight = counts_ref[...].astype(jnp.float32)
    line = lax.broadcasted_iota(jnp.int32, (8, rows), 0)
    facts = jnp.where(
        line == first % 8,
        (slot >> 8).astype(jnp.float32),
        jnp.where(
            line == first % 8 + 1,
            (slot & 255).astype(jnp.float32),
            jnp.where(line == first % 8 + 2, weight, 0.0),
        ),
    ).astype(jnp.bfloat16)
    places = lax.broadcasted_iota(jnp.int32, (padded, rows), 0)
    beyond = (lax.broadcasted_iota(jnp.int32, (8, columns), 0) == first % 8) & (
        lax.broadcasted_iota(jnp.int32, (8, columns), 1) >= capacity
    )
    blocks = []
    for j in range(peers):
        match = places == jnp.where(relative == j, rank, -1)
        named = dot_rows(facts, jnp.where(match, 1.0, 0.0).astype(jnp.bfloat16))
        named = jnp.concatenate([named, jnp.zeros((8, columns - padded), jnp.float32)], axis=1)
        named = jnp.where(beyond, 255.0, named)
        scaled = jnp.where(match, weight, 0.0).astype(jnp.bfloat16)
        body = jnp.dot(scaled, vis_ref[...], preferred_element_type=jnp.float32)
        blocks += [body[: size - 8], body[size - 8 : size] + named]
        if j % 2:
            out_refs[j // 2][...] = jnp.concatenate(blocks, axis=0).astype(jnp.bfloat16)
            blocks = []
    ahead.wait()


def dot_rows(left, right):
    return lax.dot_general(
        left, right, (((1,), (1,)), ((), ())), preferred_element_type=jnp.float32
    )


def groups(peers):
    chips = peers // 2
    return (
        [2 * k + 1 for k in range(chips)],
        [2 * k for k in range(chips) if k & (chips // 2)],
        [2 * k for k in range(chips) if not k & (chips // 2)],
    )


def load_kernel(peers, chunk, beam_ref, start_ref, after_ref, *refs):
    outs, done_ref, buffer, sems = (refs[:3], refs[3:6], refs[6:9]), refs[9], refs[10], refs[11]
    done_ref[...] = jnp.zeros(done_ref.shape, done_ref.dtype)
    steps = beam_ref.shape[0] // chunk
    ahead = start_ref.shape[0] // chunk
    slots = buffer.shape[0]
    width = beam_ref.shape[1] // peers
    me = lax.axis_index("pair")

    def copy(step):
        return pltpu.make_async_copy(
            beam_ref.at[pl.ds(step * chunk, chunk)],
            buffer.at[step % slots],
            sems.at[step % slots],
        )

    for step in range(ahead, min(ahead + slots, steps)):
        copy(step).start()
    for step in range(steps):
        if step < ahead:
            source = start_ref.at[pl.ds(step * chunk, chunk)]
        else:
            copy(step).wait()
            source = buffer.at[step % slots]

        @pl.loop(0, chunk // 32)
        def _(line):
            at = pl.multiple_of(line * 32, 32)
            for (high_ref, again_ref, rest_ref), owners in zip(outs, groups(peers)):
                for i, j in enumerate(owners):
                    lane = pl.multiple_of((me ^ j) * width, width)
                    value = source[pl.ds(at, 32), pl.ds(lane, width)]
                    high = value.astype(jnp.bfloat16)
                    rest = value - high.astype(jnp.float32)
                    to = (pl.ds(step * chunk + at, 32), slice(i * width, (i + 1) * width))
                    high_ref[to] = high
                    again_ref[to] = (high * BEAM).astype(SMALL)
                    rest_ref[to] = (rest * BEAM_REST).astype(SMALL)

        if ahead <= step < steps - slots:
            copy(step + slots).start()


def add_up(capacity, blocks, base_dev, write):
    first, size = block_rows(capacity)
    slots, weights = [], []
    for block in blocks:
        facts = block[size - 8 :].T[:size]
        high = facts[:, first % 8 : first % 8 + 1]
        low = facts[:, first % 8 + 1 : first % 8 + 2]
        slots.append((high * 256.0 + low).astype(jnp.int32))
        weights.append(jnp.broadcast_to(facts[:, first % 8 + 2 : first % 8 + 3], (size, 128)))
    rows = jnp.concatenate(blocks, axis=0).T
    weights = jnp.concatenate(weights, axis=0).T[:16]
    slots = jnp.concatenate(slots, axis=0)
    left = jnp.concatenate([rows, weights], axis=0).astype(jnp.bfloat16)
    tile = 512
    places = lax.broadcasted_iota(jnp.int32, (slots.shape[0], tile), 1)
    for n in range(base_dev // tile):
        match = jnp.where(places == slots - n * tile, 1.0, 0.0).astype(jnp.bfloat16)
        write(n * tile, tile, jnp.dot(left, match, preferred_element_type=jnp.float32))


def pass_kernel(capacity, *refs):
    _, size = block_rows(capacity)
    blocks = [piece[...].astype(jnp.float32)[size:] for piece in refs[:-2]]
    refs[-1][...] = jnp.concatenate(blocks, axis=0).astype(jnp.bfloat16)


def direct_kernel(capacity, *refs):
    _, size = block_rows(capacity)
    sums_ref = refs[-1]

    def write(at, tile, sums):
        sums_ref[:, at : at + tile] = sums

    blocks = [piece[...].astype(jnp.float32)[:size] for piece in refs[:-2]]
    add_up(capacity, blocks, sums_ref.shape[1], write)


def stack_kernel(capacity, mwin, blocks_ref, direct_ref, *refs):
    held, (left_ref, small_ref, *send_refs) = refs[:3], refs[3:]
    _, size = block_rows(capacity)
    columns = blocks_ref.shape[1]
    base_dev = direct_ref.shape[1]
    half = columns // (2 * mwin)

    def write(at_n, tile, sums):
        sums = sums + direct_ref[:, at_n : at_n + tile]
        stacked = sums[:columns] * (1.0 / jnp.maximum(sums[columns : columns + 1], 1.0))
        high = stacked.astype(jnp.bfloat16)
        rest = (stacked - high.astype(jnp.float32)) * STACK_REST
        again = stacked * STACK
        straight = slice(at_n, at_n + tile)
        crossed = slice(base_dev + at_n, base_dev + at_n + tile)
        for m in range(mwin):
            at = 2 * half * m
            real, imag = slice(at, at + half), slice(at + half, at + 2 * half)
            upper, lower = slice(0, half), slice(half, 2 * half)
            for value, to in (
                (high, left_ref.at[m]),
                (rest, small_ref.at[m, 0]),
                (again, small_ref.at[m, 1]),
            ):
                to[upper, straight] = value[real].astype(to.dtype)
                to[lower, straight] = value[imag].astype(to.dtype)
                to[upper, crossed] = value[imag].astype(to.dtype)
                to[lower, crossed] = (-value[real]).astype(to.dtype)

    values = blocks_ref[...].astype(jnp.float32)
    blocks = [values[i : i + size] for i in range(0, values.shape[0], size)]
    add_up(capacity, blocks, base_dev, write)
    project(left_ref, small_ref, *held, *send_refs)


def project(left_ref, small_ref, high_ref, again_ref, rest_ref, *out_refs):
    mwin, half, depth = left_ref.shape
    width = out_refs[0].shape[2]
    for m in range(mwin):
        planes = slice(m * depth, (m + 1) * depth)
        rough = jnp.dot(left_ref[m], high_ref[planes], preferred_element_type=jnp.float32)
        fine = jnp.dot(
            small_ref[m, 0], again_ref[planes], preferred_element_type=jnp.float32
        ) + jnp.dot(small_ref[m, 1], rest_ref[planes], preferred_element_type=jnp.float32)
        total = rough + fine * (1.0 / (BEAM * STACK_REST))
        blocks = [out_ref.at[i] for out_ref in out_refs for i in range(out_ref.shape[0])]
        for i, block_ref in enumerate(blocks):
            block_ref[m * half : (m + 1) * half] = total[:, i * width : (i + 1) * width]


def keep_kernel(*refs):
    project(*refs[:5], refs[-1])


def staged(visibility, pair_counts, owner_ids, slot_ids, beam):
    peers = lax.axis_size("pair")
    chips = peers // 2
    rows, columns = visibility.shape[1:]
    capacity = 2 * rows // peers + 4
    mwin, _, base_dev, modes = beam.shape[1:]
    width = modes // peers
    _, size = block_rows(capacity)
    vmem = pl.BlockSpec(memory_space=pltpu.VMEM)
    anywhere = pl.BlockSpec(memory_space=pl.ANY)
    block = jax.ShapeDtypeStruct((2 * size, columns), jnp.bfloat16)
    facts = [value.reshape(1, rows) for value in (pair_counts, owner_ids, slot_ids)]
    chunk = 128
    planes = beam.reshape(mwin * 2 * base_dev, modes)
    *pieces, start = pl.pallas_call(
        functools.partial(pack_kernel, peers, capacity),
        out_shape=[block] * chips + [pltpu.VMEM((AHEAD * chunk, modes), jnp.float32)],
        in_specs=[anywhere] * 5,
        out_specs=[vmem] * (chips + 1),
        scratch_shapes=[pltpu.VMEM((rows, columns), jnp.bfloat16)]
        + [pltpu.VMEM((1, rows), jnp.int32)] * 3
        + [pltpu.SemaphoreType.DMA((5,))],
        compiler_params=pltpu.CompilerParams(vmem_limit_bytes=8 * MIB),
        name="pack",
    )(
        *[
            pltpu.with_memory_space_constraint(value, pltpu.HBM)
            for value in (visibility[0], *facts, planes)
        ]
    )
    order = [k for k in range(1, chips) if k & (chips // 2)] + [
        k for k in range(1, chips) if not k & (chips // 2)
    ]
    moved = {k: swap(pieces[k], "pair", 2 * k) for k in order}
    *held, loaded = pl.pallas_call(
        functools.partial(load_kernel, peers, chunk),
        out_shape=tuple(
            pltpu.VMEM((planes.shape[0], len(owners) * width), dtype)
            for owners in groups(peers)
            for dtype in (jnp.bfloat16, SMALL, SMALL)
        )
        + (jax.ShapeDtypeStruct((8, 128), jnp.float32),),
        in_specs=[anywhere, vmem, anywhere],
        out_specs=(vmem,) * 10,
        scratch_shapes=[
            pltpu.VMEM((16, chunk, modes), jnp.float32),
            pltpu.SemaphoreType.DMA((16,)),
        ],
        compiler_params=pltpu.CompilerParams(vmem_limit_bytes=12 * MIB),
        cost_estimate=pl.CostEstimate(
            flops=0, bytes_accessed=8 * planes.size, transcendentals=0
        ),
        name="load",
    )(planes, pltpu.with_memory_space_constraint(start, pltpu.VMEM), pieces[0])
    held = [pltpu.with_memory_space_constraint(part, pltpu.VMEM) for part in held]

    def products(count):
        return jax.ShapeDtypeStruct((count, columns, width), jnp.float32)

    def cost(count):
        flops = 6 * mwin * 2 * (columns // mwin) * base_dev * count * width
        return pl.CostEstimate(flops=flops, bytes_accessed=0, transcendentals=0)

    received = [pieces[0]] + [moved[k] for k in order]
    passed = pl.pallas_call(
        functools.partial(pass_kernel, capacity),
        out_shape=jax.ShapeDtypeStruct((chips * size, columns), jnp.bfloat16),
        in_specs=[vmem] * chips + [anywhere],
        out_specs=vmem,
        compiler_params=pltpu.CompilerParams(vmem_limit_bytes=8 * MIB),
        name="pass",
    )(*received, loaded)
    got = swap(passed, "pair", 1)
    direct = pl.pallas_call(
        functools.partial(direct_kernel, capacity),
        out_shape=pltpu.VMEM((columns + 16, base_dev), jnp.float32),
        in_specs=[vmem] * chips + [anywhere],
        out_specs=vmem,
        compiler_params=pltpu.CompilerParams(vmem_limit_bytes=12 * MIB),
        cost_estimate=cost(1),
        name="direct",
    )(*received, loaded)
    left, small, near_send, far_send = pl.pallas_call(
        functools.partial(stack_kernel, capacity, mwin),
        out_shape=(
            pltpu.VMEM((mwin, columns // mwin, 2 * base_dev), jnp.bfloat16),
            pltpu.VMEM((mwin, 2, columns // mwin, 2 * base_dev), SMALL),
            products(chips // 2),
            products(chips // 2),
        ),
        in_specs=[vmem] * 5,
        out_specs=(vmem,) * 4,
        compiler_params=pltpu.CompilerParams(vmem_limit_bytes=12 * MIB),
        cost_estimate=cost(chips),
        name="stack",
    )(got, pltpu.with_memory_space_constraint(direct, pltpu.VMEM), *held[:3])
    far_got, near_got = swap(far_send, "pair", 1), swap(near_send, "pair", 1)
    left, small = [pltpu.with_memory_space_constraint(part, pltpu.VMEM) for part in (left, small)]
    summed, after = {}, []
    for name, got, parts, owners in zip(
        ("far", "near"), (far_got, near_got), (held[3:6], held[6:9]), groups(peers)[1:]
    ):
        keep = pl.pallas_call(
            keep_kernel,
            out_shape=products(len(owners)),
            in_specs=[vmem] * 5 + [anywhere] * len(after),
            out_specs=vmem,
            compiler_params=pltpu.CompilerParams(vmem_limit_bytes=12 * MIB),
            cost_estimate=cost(len(owners)),
            name=name,
        )(left, small, *parts, *after)
        for i, j in enumerate(owners):
            k = j // 2
            summed[k] = keep[i] + got[i]
            if k:
                summed[k] = summed[k].astype(jnp.bfloat16)
            if k & (chips // 2):
                after.append(summed[k])
    amplitudes = summed[0]
    for k in order[-2::-1] + order[-1:]:
        if not k & (chips // 2):
            amplitudes = lax.optimization_barrier(amplitudes)
        partial = amplitudes
        last = swap(summed[k], "pair", 2 * k)
        amplitudes = partial + last.astype(jnp.float32)
    partial, last = lax.optimization_barrier((partial, last))
    modes_out = partial + last.astype(jnp.float32)
    sets = columns // (2 * mwin)
    power = jnp.sum((amplitudes * amplitudes).reshape(mwin, 2 * sets, width), axis=1)
    terms = [power] + [swap(power, "chan", d) for d in range(1, lax.axis_size("chan"))]
    while len(terms) > 1:
        terms = [one + other for one, other in zip(terms[::2], terms[1::2])]
    power = terms[0]
    power = power / (lax.axis_size("chan") * sets)
    shaped = modes_out.reshape(mwin, 2, sets, width).transpose(3, 0, 1, 2)
    return shaped[None], power.T


def plain(visibility, pair_counts, owner_ids, slot_ids, beam):
    peers = lax.axis_size("pair")
    pair_rows = pair_counts.shape[0]
    capacity = 2 * pair_rows // peers + 4
    owner = owner_ids[:, 0]
    order = jnp.argsort(owner, stable=True)
    sorted_owner = owner[order]
    owner_list = jnp.arange(peers, dtype=jnp.int32)
    first_at = jnp.searchsorted(sorted_owner, owner_list, side="left")
    last_at = jnp.searchsorted(sorted_owner, owner_list, side="right")
    ranks = jnp.arange(capacity, dtype=jnp.int32)
    valid = ranks[None, :] < (last_at - first_at)[:, None]
    where_at = jnp.clip(first_at[:, None] + ranks[None, :], 0, pair_rows - 1)
    picked = order[where_at]
    weights = jnp.where(valid, pair_counts[picked], 0)
    offsets = jnp.where(valid, slot_ids[picked], 0)
    rows = visibility[0][picked]
    weighted = (rows.astype(jnp.float32) * weights[:, :, None].astype(jnp.float32)).astype(
        jnp.bfloat16
    )
    got_rows, got_offsets, got_weights = (
        lax.all_to_all(weighted, "pair", split_axis=0, concat_axis=0, tiled=True),
        lax.all_to_all(offsets, "pair", split_axis=0, concat_axis=0, tiled=True),
        lax.all_to_all(weights, "pair", split_axis=0, concat_axis=0, tiled=True),
    )
    columns = got_rows.shape[2]
    got_rows = got_rows.reshape(peers * capacity, columns)
    got_offsets = got_offsets.reshape(peers * capacity)
    got_weights = got_weights.reshape(peers * capacity).astype(jnp.float32)
    beam_local = beam[0]
    mwin = beam_local.shape[0]
    base_dev = beam_local.shape[2]
    sets = columns // (2 * mwin)
    matches = jnp.arange(base_dev, dtype=jnp.int32)[:, None] == got_offsets[None, :]
    numer = jnp.dot(matches.astype(jnp.bfloat16), got_rows, preferred_element_type=jnp.float32)
    denom = jnp.sum(jnp.where(matches, got_weights[None, :], 0.0), axis=1)
    stacked = numer / jnp.maximum(denom, 1.0)[:, None]
    stacked = stacked.reshape(base_dev, mwin, 2 * sets)
    swapped = jnp.concatenate([stacked[:, :, sets:], -stacked[:, :, :sets]], axis=2)
    right = jnp.stack([stacked, swapped], axis=0)
    amplitudes = lax.psum_scatter(
        jnp.einsum(
            "mrbk,rbmc->kmc",
            beam_local,
            right,
            precision=lax.Precision.HIGHEST,
            preferred_element_type=jnp.float32,
        ),
        "pair",
        scatter_dimension=0,
        tiled=True,
    )
    power_local = jnp.sum(amplitudes * amplitudes, axis=2)
    total_power = lax.psum(power_local, "chan")
    mode_power = total_power / (lax.axis_size("chan") * sets)
    shaped = amplitudes.reshape(amplitudes.shape[0], mwin, 2, sets)
    return (shaped[None], mode_power)


def power_of_two(value):
    return value & (value - 1) == 0


def per_device(visibility, pair_counts, owner_ids, slot_ids, beam):
    peers, channels = lax.axis_size("pair"), lax.axis_size("chan")
    rows, columns = visibility.shape[1:]
    mwin, _, base_dev, modes = beam.shape[1:]
    capacity = 2 * rows // peers + 4
    fits = (
        1 < peers <= 8
        and power_of_two(peers)
        and power_of_two(channels)
        and rows % 128 == 0
        and columns % 128 == 0
        and capacity + 8 <= columns
        and base_dev % 512 == 0
        and modes % (128 * peers) == 0
        and columns % (32 * mwin) == 0
    )
    return (staged if fits else plain)(visibility, pair_counts, owner_ids, slot_ids, beam)


def solution(mesh):
    in_specs = (
        P("chan", "pair", None),
        P("pair"),
        P("pair", None),
        P("pair"),
        P("chan", None, None, "pair", None),
    )
    out_specs = (P("chan", "pair", None, None, None), P("pair", None))
    return jax.shard_map(
        per_device, mesh=mesh, in_specs=in_specs, out_specs=out_specs, check_vma=False
    )
```
